512 devices in a mesh: dom: 32 (over x_lo, y, core), blk: 16 (over x_hi, z).
Axes of the slice: x: 4 (x_hi: 2, x_lo: 2; x = x_hi * 2 + x_lo), y: 8, z: 8, core: 2. Of those that a mesh axis runs over, the one named last changes fastest.
Arguments:
- features: bfloat16 [196608, 256], P(('dom', 'blk')), may hold values from -6 to 6
- weight: bfloat16 [256, 256], replicated, may hold values from -0.375 to 0.375
- bias: float32 [256], replicated, may hold values from -3 to 3
- cotangent: bfloat16 [196608, 256], P(('dom', 'blk')), may hold values from -6 to 6
- in_tiles: bfloat16 [32, 16, 16, 4, 128, 128], P('dom', 'blk'), may hold values from -0.125 to 0.125
- in_pos: int32 [32, 16, 16, 4], P('dom', 'blk'), may hold values from 0 to 8, as said below
- in_count: int32 [32, 16, 16], P('dom', 'blk'), may hold values from 1 to 4, as said below
- cut_tiles: bfloat16 [32, 16, 32, 128, 128], P('dom', 'blk'), may hold values from -0.125 to 0.125
- send_blk: int32 [32, 16, 32], P('dom', 'blk'), may hold values from 0 to 2
- send_live: int32 [32, 16, 32], P('dom', 'blk'), may hold values from 0 to 1, as said below
- recv_dst: int32 [32, 16, 32], P('dom', 'blk'), may hold values from 0 to 2
Outputs:
- hidden: bfloat16 [196608, 256], P(('dom', 'blk'))
- grad_features: bfloat16 [196608, 256], P(('dom', 'blk'))
The draws below stay inside these ranges and needn't reach their ends.
Inputs may be any that keep to these rules, and one draw needn't show every extreme that they name: The first in_count[p, b, c] entries of in_pos[p, b, c] are distinct; later slots, and their tiles, are ignored. in_count[p, b, b] = 4. send_live[p, b, p] = 0 and send_live[p, b, q] = 1 for q = (p + 1) modulo the number of parts. Where it is 0 the slot's cut tile, send_blk and recv_dst are ignored.
All inputs are finite; a program needn't handle non-finite values.
Results may differ from the reference program's by a relative error of at most 0.007.
Values may be sent and summed in bfloat16 or wider, within the bound.
No kernel may reach another device: no remote copies, remote signals or barrier semaphores. Data moves between devices by JAX's collectives and lax.ppermute only.
A program may use at most 64 MiB of HBM per device.

```python
import jax
import jax.numpy as jnp
from jax import lax

F = 256
TB = 128
RB = 3
STEP_CAP = 4
NODES = 196608
N_DOM = 32
N_BLK = 16


def draw_in_pos(key, part):
    key = jax.random.fold_in(key, 11)
    position_count = RB * RB
    scores = jax.random.randint(key, (N_DOM, N_BLK, N_BLK, position_count), 0, 1 << 20)
    ranked = scores * position_count + jnp.arange(position_count, dtype=jnp.int32)
    ordering = jnp.argsort(ranked, axis=-1)
    return ordering[..., :STEP_CAP].astype(jnp.int32)


def draw_in_count(key, part):
    key = jax.random.fold_in(key, 12)
    subkeys = jax.random.split(key, 3)
    base_count = jax.random.randint(subkeys[0], (N_DOM, N_BLK, N_BLK), 1, 4)
    heavy_device = jax.random.randint(subkeys[1], (N_DOM, N_BLK, 1), 0, 2)
    extra_count = jax.random.randint(subkeys[2], (N_DOM, N_BLK, N_BLK), 0, 3)
    counted = jnp.minimum(base_count + heavy_device * extra_count, STEP_CAP)
    diagonal = jnp.arange(N_BLK)[:, None] == jnp.arange(N_BLK)[None, :]
    return jnp.where(diagonal[None], STEP_CAP, counted).astype(jnp.int32)


def draw_send_live(key, part):
    key = jax.random.fold_in(key, 13)
    rolled = jax.random.randint(key, (N_DOM, N_BLK, N_DOM), 0, 8)
    live_flags = jnp.where(rolled > 0, 1, 0)
    source_part = jnp.arange(N_DOM)[:, None, None]
    target_part = jnp.arange(N_DOM)[None, None, :]
    live_flags = jnp.where(target_part == source_part, 0, live_flags)
    live_flags = jnp.where(target_part == (source_part + 1) % N_DOM, 1, live_flags)
    return live_flags.astype(jnp.int32)


def with_ends(array, stream_key, low, largest):
    dims = array.shape
    place = [jax.random.randint(jax.random.fold_in(stream_key, axis), (), 0, dims[axis]) for axis in range(len(dims))]
    array = array.at[tuple(place)].set(low)
    longest = dims.index(max(dims))
    place[longest] = (place[longest] + 1) % dims[longest]
    return array.at[tuple(place)].set(largest)


def level_of(rng, dims, pieces, low, top_value):
    loudness, own = 1.0, jax.random.fold_in(rng, 6)
    for dim, blocks in pieces:
        draws = jnp.exp(jax.random.uniform(jax.random.fold_in(own, dim), (blocks,), jnp.float32, low / len(pieces), top_value / len(pieces)))
        loudness = loudness * jnp.repeat(draws, dims[dim] // blocks).reshape([-1 if axis == dim else 1 for axis in range(len(dims))])
    return loudness


def centred(own_key, shape, deviation, limit, cuts=(), kind=jnp.bfloat16):
    values = jax.random.normal(own_key, shape, jnp.float32) * deviation
    if len(cuts) > 0:
        values = level_of(own_key, shape, cuts, -0.22, 0.18) * values
    return jnp.clip(values, min=-limit, max=limit).astype(kind)


def setup_inputs(seed: int = 0) -> dict:
    streams_of = jax.random.split(jax.random.key(seed), 12)
    features = centred(streams_of[0], (NODES, F), 1.0, 6.0, ((0, 512),))
    weight = centred(streams_of[1], (F, F), F ** -0.5, 0.375)
    bias = centred(streams_of[2], (F,), 0.5, 3.0, (), jnp.float32)
    cotangent = centred(streams_of[3], (NODES, F), 1.0, 6.0, ((0, 512),))
    in_tiles = centred(streams_of[4], (N_DOM, N_BLK, N_BLK, STEP_CAP, TB, TB), (TB * N_BLK) ** -0.5, 0.125, ((0, 32), (1, 16)))
    in_pos = draw_in_pos(jax.random.fold_in(streams_of[11], 71), 0)
    in_count = draw_in_count(jax.random.fold_in(streams_of[11], 71), 0)
    cut_tiles = centred(streams_of[7], (N_DOM, N_BLK, N_DOM, TB, TB), (TB * N_BLK) ** -0.5, 0.125, ((0, 32), (1, 16)))
    send_blk = with_ends(jax.random.randint(streams_of[8], (N_DOM, N_BLK, N_DOM), 0, RB), jax.random.fold_in(streams_of[8], 1), 0, RB - 1).astype(jnp.int32)
    send_live = draw_send_live(jax.random.fold_in(streams_of[11], 71), 0)
    recv_dst = with_ends(jax.random.randint(streams_of[10], (N_DOM, N_BLK, N_DOM), 0, RB), jax.random.fold_in(streams_of[10], 1), 0, RB - 1).astype(jnp.int32)
    return dict(features=features, weight=weight, bias=bias, cotangent=cotangent, in_tiles=in_tiles, in_pos=in_pos, in_count=in_count, cut_tiles=cut_tiles, send_blk=send_blk, send_live=send_live, recv_dst=recv_dst)


def silu_parts(preact):
    sigmoid = 1.0 / (1.0 + jnp.exp(-preact))
    return preact * sigmoid, sigmoid * (1.0 + preact * (1.0 - sigmoid))


def reference(features, weight, bias, cotangent, in_tiles, in_pos, in_count, cut_tiles, send_blk, send_live, recv_dst):
    feat_width = features.shape[1]
    highest = lax.Precision.HIGHEST
    projected = jnp.dot(features, weight, preferred_element_type=jnp.float32).astype(jnp.bfloat16)
    proj_blocks = projected.reshape(N_DOM, N_BLK, RB, TB, feat_width)
    slot_ids = jnp.arange(STEP_CAP, dtype=jnp.int32)
    block_ids = jnp.arange(RB, dtype=jnp.int32)
    part_ids = jnp.arange(N_DOM, dtype=jnp.int32)
    device_ids = jnp.arange(N_BLK, dtype=jnp.int32)
    slot_live = slot_ids < in_count[..., None]
    target_index = in_pos // RB
    source_index = in_pos % RB
    target_onehot = ((target_index[..., None] == block_ids) & slot_live[..., None]).astype(jnp.float32)
    source_onehot = ((source_index[..., None] == block_ids) & slot_live[..., None]).astype(jnp.float32)
    cut_live = send_live.astype(jnp.float32)
    recv_onehot = (recv_dst[..., None] == block_ids).astype(jnp.float32)
    send_onehot = (send_blk[..., None] == block_ids).astype(jnp.float32)

    def forward_part(part_id):
        own_rows = proj_blocks[part_id]
        source_rows = own_rows[device_ids[None, :, None], source_index[part_id]]
        products = jnp.einsum("bckxy,bckyf->bckxf", in_tiles[part_id].astype(jnp.float32), source_rows.astype(jnp.float32), precision=highest)
        intra_sum = jnp.einsum("bckr,bckxf->brxf", target_onehot[part_id], products, precision=highest)
        sent_rows = proj_blocks[part_ids[:, None], device_ids[None, :], send_blk[:, :, part_id]]
        sent_rows = sent_rows.astype(jnp.float32) * cut_live[:, :, part_id][..., None, None]
        cross_terms = jnp.einsum("bpxy,pbyf->bpxf", cut_tiles[part_id].astype(jnp.float32), sent_rows, precision=highest)
        cross_sum = jnp.einsum("bpr,bpxf->brxf", recv_onehot[part_id], cross_terms, precision=highest)
        return intra_sum + cross_sum

    aggregate = lax.map(forward_part, part_ids).reshape(N_DOM * N_BLK * RB * TB, feat_width)
    activated, derivative = silu_parts(aggregate + bias)
    hidden = activated.astype(jnp.bfloat16)
    grad_pre = (cotangent.astype(jnp.float32) * derivative).astype(jnp.bfloat16)
    grad_blocks = grad_pre.reshape(N_DOM, N_BLK, RB, TB, feat_width)

    def backward_part(part_id):
        own_rows = grad_blocks[part_id]
        target_rows = own_rows[device_ids[:, None, None], target_index[part_id]]
        products = jnp.einsum("bckxy,bckxf->bckyf", in_tiles[part_id].astype(jnp.float32), target_rows.astype(jnp.float32), precision=highest)
        intra_sum = jnp.einsum("bckr,bckyf->cryf", source_onehot[part_id], products, precision=highest)
        far_rows = grad_blocks[part_ids[:, None], device_ids[None, :], recv_dst[:, :, part_id]]
        far_tiles = cut_tiles[:, :, part_id].astype(jnp.float32)
        cross_terms = jnp.einsum("qbxy,qbxf->qbyf", far_tiles, far_rows.astype(jnp.float32), precision=highest)
        cut_back = lax.optimization_barrier(cross_terms.astype(jnp.bfloat16)).astype(jnp.float32)
        weights_live = jnp.transpose(send_onehot[part_id] * cut_live[part_id][..., None], (1, 0, 2))
        cross_sum = jnp.einsum("qbr,qbyf->bryf", weights_live, cut_back, precision=highest)
        return intra_sum + cross_sum

    back_sum = lax.map(backward_part, part_ids).reshape(N_DOM * N_BLK * RB * TB, feat_width)
    back_rows = back_sum.astype(jnp.bfloat16)
    grad_features = jnp.dot(back_rows, weight.T, preferred_element_type=jnp.float32).astype(jnp.bfloat16)
    return hidden, grad_features
```

```python
import jax
import jax.numpy as jnp
from jax import lax
from jax.experimental import pallas as pl
from jax.experimental.pallas import tpu as pltpu
from jax.sharding import PartitionSpec as P

BF, F32, I32 = jnp.bfloat16, jnp.float32, jnp.int32
TILE = 128
FAR = 2
STEPS = 4
VMEM_LIMIT = 40 * 1024 * 1024


def spec(space):
    return pl.BlockSpec(memory_space=space)


def silu_parts(preact):
    sigmoid = 1.0 / (1.0 + jnp.exp(-preact))
    return (preact * sigmoid, sigmoid * (1.0 + preact * (1.0 - sigmoid)))


def project_kernel(blk_ref, live_ref, features_ref, weight_ref, projected_ref, outgoing_ref):
    projected_ref[...] = jnp.dot(
        features_ref[...], weight_ref[...], preferred_element_type=F32
    ).astype(BF)

    def fill(part, carried):
        @pl.when(live_ref[part] > 0)
        def _():
            row = pl.multiple_of(blk_ref[part] * TILE, TILE)
            outgoing_ref[part] = projected_ref[pl.ds(row, TILE), :]

        @pl.when(live_ref[part] <= 0)
        def _():
            outgoing_ref[part] = jnp.zeros(outgoing_ref.shape[1:], BF)

        return carried

    lax.fori_loop(0, outgoing_ref.shape[0], fill, 0)


def spread_kernel(ring, blocks, pos_ref, count_ref, dst_ref, place_ref, tiles_ref, cut_ref, *outs):
    ahead, back = outs[:ring], outs[ring : 2 * ring]
    cut_ahead, cut_back = outs[2 * ring :]
    rows = blocks * TILE
    place = place_ref[0]
    for offset in range(ring):
        ahead[offset][...] = jnp.zeros(ahead[offset].shape, BF)
        back[offset][...] = jnp.zeros(back[offset].shape, BF)
        spot = lax.rem(place + offset, ring)
        for half in range(FAR):
            source = half * ring + spot

            def put(slot, carried, offset=offset, half=half, source=source):
                position = pos_ref[source * tiles_ref.shape[1] + slot]
                target = pl.multiple_of(position // blocks * TILE, TILE)
                origin = pl.multiple_of(half * rows + position % blocks * TILE, TILE)
                tile = tiles_ref[source, slot]
                ahead[offset][pl.ds(target, TILE), pl.ds(origin, TILE)] = tile
                back[offset][pl.ds(origin, TILE), pl.ds(target, TILE)] = (
                    tile.astype(F32).T.astype(BF)
                )
                return carried

            lax.fori_loop(0, count_ref[source], put, 0)
    cut_ahead[...] = jnp.zeros(cut_ahead.shape, BF)
    cut_back[...] = jnp.zeros(cut_back.shape, BF)

    def put_cut(part, carried):
        target = pl.multiple_of(dst_ref[part] * TILE, TILE)
        origin = pl.multiple_of(part * TILE, TILE)
        tile = cut_ref[part]
        cut_ahead[pl.ds(target, TILE), pl.ds(origin, TILE)] = tile
        cut_back[pl.ds(origin, TILE), pl.ds(target, TILE)] = tile.astype(F32).T.astype(BF)
        return carried

    lax.fori_loop(0, cut_ref.shape[0], put_cut, 0)


def middle_kernel(
    sum_ref,
    mat_ref,
    low_ref,
    high_ref,
    bias_ref,
    cotangent_ref,
    ahead_ref,
    far_ref,
    back_ref,
    hidden_ref,
    grad_ref,
    terms_ref,
    total,
):
    step = pl.program_id(0)
    rows = sum_ref.shape[0]
    width = sum_ref.shape[1]

    @pl.when(step == 0)
    def _():
        total[...] = (
            sum_ref[...]
            + jnp.dot(mat_ref[:, :rows], low_ref[...], preferred_element_type=F32)
            + jnp.dot(mat_ref[:, rows:], high_ref[...], preferred_element_type=F32)
        )

    @pl.when(step < STEPS)
    def _():
        arrived = far_ref[...].reshape(-1, width)
        total[...] += jnp.dot(ahead_ref[...], arrived, preferred_element_type=F32)

    @pl.when(step == STEPS - 1)
    def _():
        activated, derivative = silu_parts(total[...] + bias_ref[...])
        hidden_ref[...] = activated.astype(BF)
        grad_ref[...] = (cotangent_ref[...].astype(F32) * derivative).astype(BF)

    @pl.when(step >= STEPS)
    def _():
        product = jnp.dot(back_ref[...], grad_ref[...], preferred_element_type=F32)
        terms_ref[...] = product.astype(BF).reshape(terms_ref.shape)


def last_kernel(blk_ref, live_ref, own_ref, other_ref, weight_ref, arrived_ref, out_ref, total):
    step = pl.program_id(0)
    chunk = arrived_ref.shape[0]

    @pl.when(step == 0)
    def _():
        total[...] = own_ref[...] + other_ref[...].astype(F32)

    def add(slot, carried):
        part = step * chunk + slot

        @pl.when(live_ref[part] > 0)
        def _():
            row = pl.ds(pl.multiple_of(blk_ref[part] * TILE, TILE), TILE)
            total[row, :] += arrived_ref[slot].astype(F32)

        return carried

    lax.fori_loop(0, chunk, add, 0)

    @pl.when(step == STEPS - 1)
    def _():
        out_ref[...] = lax.dot_general(
            total[...].astype(BF),
            weight_ref[...],
            (((1,), (1,)), ((), ())),
            preferred_element_type=F32,
        ).astype(BF)


def on_device(
    features,
    weight,
    bias,
    cotangent,
    in_tiles,
    in_pos,
    in_count,
    cut_tiles,
    send_blk,
    send_live,
    recv_dst,
):
    rows, width = features.shape
    blocks = rows // TILE
    peers = lax.axis_size("blk")
    parts = lax.axis_size("dom")
    ring = peers // FAR
    reach = ring // 2
    me = lax.axis_index("blk")
    place, half = me % ring, me // ring
    smem, vmem = spec(pltpu.SMEM), spec(pltpu.VMEM)
    params = pltpu.CompilerParams(vmem_limit_bytes=VMEM_LIMIT)
    send_to, is_live, dst = send_blk[0, 0], send_live[0, 0], recv_dst[0, 0]

    def along_ring(value, by):
        moves = [
            (side * ring + spot, side * ring + (spot + by) % ring)
            for side in range(FAR)
            for spot in range(ring)
        ]
        return lax.ppermute(value, "blk", moves)

    def across(value):
        return lax.ppermute(value, "blk", [(i, (i + ring) % peers) for i in range(peers)])

    def product(left, right):
        return jnp.dot(left, right, preferred_element_type=F32)

    projected, outgoing = pl.pallas_call(
        project_kernel,
        out_shape=(
            jax.ShapeDtypeStruct((rows, width), BF),
            jax.ShapeDtypeStruct((parts, TILE, width), BF),
        ),
        in_specs=[smem, smem, vmem, vmem],
        out_specs=(vmem, vmem),
        compiler_params=params,
        name="project",
    )(send_to, is_live, features, weight)
    incoming = lax.all_to_all(outgoing, "dom", split_axis=0, concat_axis=0, tiled=True)
    partner = across(projected)

    wide = FAR * rows
    dense = pl.pallas_call(
        lambda *refs: spread_kernel(ring, blocks, *refs),
        out_shape=tuple(
            [jax.ShapeDtypeStruct((rows, wide), BF)] * ring
            + [jax.ShapeDtypeStruct((wide, rows), BF)] * ring
            + [jax.ShapeDtypeStruct((rows, parts * TILE), BF)]
            + [jax.ShapeDtypeStruct((parts * TILE, rows), BF)]
        ),
        in_specs=[smem] * 4 + [vmem] * 2,
        out_specs=tuple([vmem] * (2 * ring + 2)),
        compiler_params=params,
        cost_estimate=pl.CostEstimate(flops=0, bytes_accessed=24 << 20, transcendentals=0),
        name="spread",
    )(
        in_pos[0, 0].reshape(-1),
        in_count[0, 0],
        dst,
        place.reshape(1),
        in_tiles[0, 0],
        cut_tiles[0, 0],
    )
    ahead, back = dense[:ring], dense[ring : 2 * ring]
    cut_ahead, cut_back = dense[2 * ring :]

    pair = jnp.where(
        half == 0,
        jnp.concatenate([projected, partner]),
        jnp.concatenate([partner, projected]),
    )
    running = product(ahead[0], pair)
    right = left = pair
    for hop in range(1, reach):
        right, left = along_ring(right, 1), along_ring(left, -1)
        running = running + product(ahead[ring - hop], right)
        running = running + product(ahead[hop], left)
    low, high = along_ring(right[:rows], 1), along_ring(left[rows:], -1)

    chunk = parts // STEPS
    whole = lambda *shape: pl.BlockSpec(shape, lambda i: (0,) * len(shape))
    first = lambda i: jnp.minimum(i, STEPS - 1)
    second = lambda i: jnp.maximum(i - STEPS, 0)
    hidden, grad_pre, terms = pl.pallas_call(
        middle_kernel,
        grid=(2 * STEPS,),
        out_shape=(
            jax.ShapeDtypeStruct((rows, width), BF),
            jax.ShapeDtypeStruct((rows, width), BF),
            jax.ShapeDtypeStruct((parts, TILE, width), BF),
        ),
        in_specs=[
            whole(rows, width),
            whole(rows, wide),
            whole(rows, width),
            whole(rows, width),
            whole(1, width),
            whole(rows, width),
            pl.BlockSpec((rows, chunk * TILE), lambda i: (0, first(i))),
            pl.BlockSpec((chunk, TILE, width), lambda i: (first(i), 0, 0)),
            pl.BlockSpec((chunk * TILE, rows), lambda i: (second(i), 0)),
        ],
        out_specs=(
            whole(rows, width),
            whole(rows, width),
            pl.BlockSpec((chunk, TILE, width), lambda i: (second(i), 0, 0)),
        ),
        scratch_shapes=[pltpu.VMEM((rows, width), F32)],
        compiler_params=params,
        name="middle",
    )(
        running,
        ahead[reach],
        low,
        high,
        bias.reshape(1, width),
        cotangent,
        cut_ahead,
        incoming,
        cut_back,
    )
    returned = lax.all_to_all(terms, "dom", split_axis=0, concat_axis=0, tiled=True)

    farthest = product(back[reach], grad_pre).astype(BF)
    low, high = along_ring(farthest[:rows], 1), along_ring(farthest[rows:], -1)
    for hop in range(reach - 1, 0, -1):
        right = product(back[hop], grad_pre)
        left = product(back[ring - hop], grad_pre)
        if hop == reach - 1:
            right = jnp.concatenate([right[:rows] + low.astype(F32), right[rows:]])
            left = jnp.concatenate([left[:rows], left[rows:] + high.astype(F32)])
        else:
            right, left = right + from_left.astype(F32), left + from_right.astype(F32)
        from_left = along_ring(right.astype(BF), 1)
        from_right = along_ring(left.astype(BF), -1)
    both = product(back[0], grad_pre) + from_left.astype(F32) + from_right.astype(F32)
    mine = jnp.where(half == 0, both[:rows], both[rows:])
    theirs = across(jnp.where(half == 0, both[rows:], both[:rows]).astype(BF))

    grad_features = pl.pallas_call(
        last_kernel,
        grid=(STEPS,),
        out_shape=jax.ShapeDtypeStruct((rows, width), BF),
        in_specs=[
            smem,
            smem,
            whole(rows, width),
            whole(rows, width),
            whole(*weight.shape),
            pl.BlockSpec((chunk, TILE, width), lambda i: (i, 0, 0)),
        ],
        out_specs=whole(rows, width),
        scratch_shapes=[pltpu.VMEM((rows, width), F32)],
        compiler_params=params,
        name="last",
    )(send_to, is_live, mine, theirs, weight, returned)
    return (hidden, grad_features)


def solution(mesh):
    in_specs = (
        P(("dom", "blk"), None),
        P(),
        P(),
        P(("dom", "blk"), None),
        P("dom", "blk", None, None, None, None),
        P("dom", "blk", None, None),
        P("dom", "blk", None),
        P("dom", "blk", None, None, None),
        P("dom", "blk", None),
        P("dom", "blk", None),
        P("dom", "blk", None),
    )
    out_specs = (P(("dom", "blk"), None), P(("dom", "blk"), None))
    return jax.shard_map(
        on_device, mesh=mesh, in_specs=in_specs, out_specs=out_specs, check_vma=False
    )
```

```python
import jax
import jax.numpy as jnp
from jax import lax
from jax.experimental import pallas as pl
from jax.experimental.pallas import tpu as pltpu
from jax.sharding import PartitionSpec as P

BF, F32 = jnp.bfloat16, jnp.float32
TILE = 128
FAR = 2
CHUNKS = 4
VMEM_LIMIT = 16 * 1024 * 1024


def spec(space):
    return pl.BlockSpec(memory_space=space)


SMEM, VMEM, HBM = spec(pltpu.SMEM), spec(pltpu.VMEM), spec(pltpu.HBM)


def call(kernel, name, out_shape, in_specs, out_specs, scratch=(), flops=0, moved=0):
    return pl.pallas_call(
        kernel,
        out_shape=out_shape,
        in_specs=in_specs,
        out_specs=out_specs,
        scratch_shapes=scratch,
        compiler_params=pltpu.CompilerParams(vmem_limit_bytes=VMEM_LIMIT),
        cost_estimate=pl.CostEstimate(flops=flops, bytes_accessed=moved, transcendentals=0),
        name=name,
    )


def in_hbm(value):
    return pltpu.with_memory_space_constraint(value, pltpu.HBM)


def product(left, right):
    return jnp.dot(left, right, preferred_element_type=F32)


def silu_parts(preact):
    sigmoid = 1.0 / (1.0 + jnp.exp(-preact))
    return (preact * sigmoid, sigmoid * (1.0 + preact * (1.0 - sigmoid)))


def project_kernel(features_hbm, weight_hbm, projected_ref, features, weight, sems):
    copies = [
        pltpu.make_async_copy(features_hbm, features, sems.at[0]),
        pltpu.make_async_copy(weight_hbm, weight, sems.at[1]),
    ]
    for copy in copies:
        copy.start()
    for copy in copies:
        copy.wait()
    projected_ref[...] = product(features[...], weight[...]).astype(BF)


def fill_kernel(blk_ref, live_ref, projected_ref, outgoing_hbm, zeros, sems):
    zeros[...] = jnp.zeros(zeros.shape, BF)
    parts = outgoing_hbm.shape[0]

    def start(part, carried):
        @pl.when(live_ref[part] > 0)
        def _():
            row = pl.multiple_of(blk_ref[part] * TILE, TILE)
            pltpu.make_async_copy(
                projected_ref.at[pl.ds(row, TILE)], outgoing_hbm.at[part], sems.at[part]
            ).start()

        @pl.when(live_ref[part] <= 0)
        def _():
            pltpu.make_async_copy(zeros, outgoing_hbm.at[part], sems.at[part]).start()

        return carried

    def wait(part, carried):
        pltpu.make_async_copy(zeros, outgoing_hbm.at[part], sems.at[part]).wait()
        return carried

    lax.fori_loop(0, parts, start, 0)
    lax.fori_loop(0, parts, wait, 0)


def spread_kernel(ring, blocks, pos_ref, count_ref, place_ref, tiles_ref, *outs):
    rows = blocks * TILE
    place = place_ref[0]
    for offset in range(ring):
        dense = outs[offset]
        dense[...] = jnp.zeros(dense.shape, BF)
        spot = lax.rem(place + offset, ring)
        for half in range(FAR):
            source = half * ring + spot

            def put(slot, carried, dense=dense, half=half, source=source):
                position = pos_ref[source * tiles_ref.shape[1] + slot]
                target = pl.multiple_of(position // blocks * TILE, TILE)
                origin = pl.multiple_of(half * rows + position % blocks * TILE, TILE)
                dense[pl.ds(target, TILE), pl.ds(origin, TILE)] = tiles_ref[source, slot]
                return carried

            lax.fori_loop(0, count_ref[source], put, 0)


def spread_cut_kernel(dst_ref, cut_ref, dense):
    dense[...] = jnp.zeros(dense.shape, BF)

    def put(part, carried):
        target = pl.multiple_of(dst_ref[part] * TILE, TILE)
        origin = pl.multiple_of(part * TILE, TILE)
        dense[pl.ds(target, TILE), pl.ds(origin, TILE)] = cut_ref[part]
        return carried

    lax.fori_loop(0, cut_ref.shape[0], put, 0)


def middle_kernel(
    sum_ref, mat_ref, low_ref, high_ref, bias_ref, cotangent_ref, cut_ref, far_ref, hidden_ref, grad_ref
):
    rows, width = sum_ref.shape
    chunk = far_ref.shape[0] // CHUNKS
    total = (
        sum_ref[...]
        + product(mat_ref[:, :rows], low_ref[...])
        + product(mat_ref[:, rows:], high_ref[...])
    )
    for piece in range(CHUNKS):
        arrived = far_ref[pl.ds(piece * chunk, chunk)].reshape(chunk * TILE, width)
        total += product(cut_ref[:, pl.ds(piece * chunk * TILE, chunk * TILE)], arrived)
    activated, derivative = silu_parts(total + bias_ref[...])
    hidden_ref[...] = activated.astype(BF)
    grad_ref[...] = (cotangent_ref[...].astype(F32) * derivative).T.astype(BF)


def terms_kernel(grad_ref, cut_ref, terms_hbm, terms, sems):
    chunk = terms.shape[0] // CHUNKS
    copies = []
    for piece in range(CHUNKS):
        columns = pl.ds(piece * chunk * TILE, chunk * TILE)
        result = product(grad_ref[...], cut_ref[:, columns]).astype(BF)
        for slot in range(chunk):
            terms[piece * chunk + slot] = result[:, slot * TILE : (slot + 1) * TILE]
        span = pl.ds(piece * chunk, chunk)
        copies.append(pltpu.make_async_copy(terms.at[span], terms_hbm.at[span], sems.at[piece]))
        copies[-1].start()
    for copy in copies:
        copy.wait()


def gather_kernel(blk_ref, live_ref, arrived_ref, total_ref):
    total_ref[...] = jnp.zeros(total_ref.shape, F32)

    def add(part, carried):
        @pl.when(live_ref[part] > 0)
        def _():
            columns = pl.ds(pl.multiple_of(blk_ref[part] * TILE, TILE), TILE)
            total_ref[:, columns] += arrived_ref[part].astype(F32)

        return carried

    lax.fori_loop(0, arrived_ref.shape[0], add, 0)


def last_kernel(own_ref, other_ref, cut_ref, weight_ref, out_ref):
    total = own_ref[...] + other_ref[...].astype(F32) + cut_ref[...]
    out_ref[...] = lax.dot_general(
        total.T.astype(BF), weight_ref[...], (((1,), (1,)), ((), ())), preferred_element_type=F32
    ).astype(BF)


def on_device(
    features,
    weight,
    bias,
    cotangent,
    in_tiles,
    in_pos,
    in_count,
    cut_tiles,
    send_blk,
    send_live,
    recv_dst,
):
    rows, width = features.shape
    blocks = rows // TILE
    peers = lax.axis_size("blk")
    parts = lax.axis_size("dom")
    ring = peers // FAR
    reach = ring // 2
    me = lax.axis_index("blk")
    place, half = me % ring, me // ring
    wide = FAR * rows
    send_to, is_live, dst = send_blk[0, 0], send_live[0, 0], recv_dst[0, 0]
    shape = jax.ShapeDtypeStruct

    def along_ring(value, by):
        moves = [
            (side * ring + spot, side * ring + (spot + by) % ring)
            for side in range(FAR)
            for spot in range(ring)
        ]
        return lax.ppermute(value, "blk", moves)

    def across(value):
        return lax.ppermute(value, "blk", [(i, (i + ring) % peers) for i in range(peers)])

    projected = call(
        project_kernel,
        "project",
        shape((rows, width), BF),
        [HBM, HBM],
        VMEM,
        [
            pltpu.VMEM(features.shape, BF),
            pltpu.VMEM(weight.shape, BF),
            pltpu.SemaphoreType.DMA((2,)),
        ],
    )(in_hbm(features), in_hbm(weight))
    partner = across(projected)
    outgoing = call(
        fill_kernel,
        "fill",
        pltpu.HBM((parts, TILE, width), BF),
        [SMEM, SMEM, VMEM],
        HBM,
        [pltpu.VMEM((TILE, width), BF), pltpu.SemaphoreType.DMA((parts,))],
    )(send_to, is_live, projected)
    incoming = lax.all_to_all(outgoing, "dom", split_axis=0, concat_axis=0, tiled=True)

    dense = call(
        lambda *refs: spread_kernel(ring, blocks, *refs),
        "spread",
        tuple([shape((rows, wide), BF)] * ring),
        [SMEM, SMEM, SMEM, VMEM],
        tuple([VMEM] * ring),
        moved=10 << 20,
    )(in_pos[0, 0].reshape(-1), in_count[0, 0], place.reshape(1), in_tiles[0, 0])
    dense_cut = call(
        spread_cut_kernel,
        "spread_cut",
        shape((rows, parts * TILE), BF),
        [SMEM, VMEM],
        VMEM,
        moved=6 << 20,
    )(dst, cut_tiles[0, 0])

    pair = jnp.where(
        half == 0,
        jnp.concatenate([projected, partner]),
        jnp.concatenate([partner, projected]),
    )
    running = product(dense[0], pair)
    right = left = pair
    for hop in range(1, reach):
        right, left = along_ring(right, 1), along_ring(left, -1)
        running = running + product(dense[ring - hop], right)
        running = running + product(dense[hop], left)
    low, high = along_ring(right[:rows], 1), along_ring(left[rows:], -1)

    hidden, grad_pre = call(
        middle_kernel,
        "middle",
        (shape((rows, width), BF), shape((width, rows), BF)),
        [VMEM] * 8,
        (VMEM, VMEM),
    )(
        running,
        dense[reach],
        low,
        high,
        bias.reshape(1, width),
        cotangent,
        dense_cut,
        incoming,
    )

    farthest = product(grad_pre, dense[reach]).astype(BF)
    low, high = along_ring(farthest[:, :rows], 1), along_ring(farthest[:, rows:], -1)
    terms = call(
        terms_kernel,
        "terms",
        pltpu.HBM((parts, width, TILE), BF),
        [VMEM, VMEM],
        HBM,
        [pltpu.VMEM((parts, width, TILE), BF), pltpu.SemaphoreType.DMA((CHUNKS,))],
        flops=2 * rows * width * parts * TILE,
        moved=6 << 20,
    )(grad_pre, dense_cut)
    returned = lax.all_to_all(terms, "dom", split_axis=0, concat_axis=0, tiled=True)
    for hop in range(reach - 1, 0, -1):
        right = product(grad_pre, dense[hop])
        left = product(grad_pre, dense[ring - hop])
        if hop == reach - 1:
            right = jnp.concatenate([right[:, :rows] + low.astype(F32), right[:, rows:]], axis=1)
            left = jnp.concatenate([left[:, :rows], left[:, rows:] + high.astype(F32)], axis=1)
        else:
            right, left = right + from_left.astype(F32), left + from_right.astype(F32)
        from_left = along_ring(right.astype(BF), 1)
        from_right = along_ring(left.astype(BF), -1)
    both = product(grad_pre, dense[0]) + from_left.astype(F32) + from_right.astype(F32)
    own = jnp.where(half == 0, both[:, :rows], both[:, rows:])
    other = across(jnp.where(half == 0, both[:, rows:], both[:, :rows]).astype(BF))
    from_cuts = call(
        gather_kernel, "gather", shape((width, rows), F32), [SMEM, SMEM, VMEM], VMEM, moved=2 << 20
    )(send_to, is_live, returned)
    grad_features = call(
        last_kernel, "last", shape((rows, width), BF), [VMEM] * 4, VMEM
    )(own, other, from_cuts, weight)
    return (hidden, grad_features)


def solution(mesh):
    in_specs = (
        P(("dom", "blk"), None),
        P(),
        P(),
        P(("dom", "blk"), None),
        P("dom", "blk", None, None, None, None),
        P("dom", "blk", None, None),
        P("dom", "blk", None),
        P("dom", "blk", None, None, None),
        P("dom", "blk", None),
        P("dom", "blk", None),
        P("dom", "blk", None),
    )
    out_specs = (P(("dom", "blk"), None), P(("dom", "blk"), None))
    return jax.shard_map(
        on_device, mesh=mesh, in_specs=in_specs, out_specs=out_specs, check_vma=False
    )
```

```python
import jax
import jax.numpy as jnp
from jax import lax
from jax.experimental import pallas as pl
from jax.experimental.pallas import tpu as pltpu
from jax.sharding import PartitionSpec as P

BF, F32 = jnp.bfloat16, jnp.float32
TILE = 128
FAR = 2
CHUNKS = 4
VMEM_LIMIT = 16 * 1024 * 1024
PAIR_COST = 100_000_000_000
CLOSE_COST = 27_800_000_000


def spec(space):
    return pl.BlockSpec(memory_space=space)


SMEM, VMEM, HBM = spec(pltpu.SMEM), spec(pltpu.VMEM), spec(pltpu.HBM)


def call(kernel, name, out_shape, in_specs, out_specs, scratch=(), flops=0, moved=0):
    return pl.pallas_call(
        kernel,
        out_shape=out_shape,
        in_specs=in_specs,
        out_specs=out_specs,
        scratch_shapes=scratch,
        compiler_params=pltpu.CompilerParams(vmem_limit_bytes=VMEM_LIMIT),
        cost_estimate=pl.CostEstimate(flops=flops, bytes_accessed=moved, transcendentals=0),
        name=name,
    )


def in_hbm(value):
    return pltpu.with_memory_space_constraint(value, pltpu.HBM)


def product(left, right):
    return jnp.dot(left, right, preferred_element_type=F32)


def silu_parts(preact):
    sigmoid = 1.0 / (1.0 + jnp.exp(-preact))
    return (preact * sigmoid, sigmoid * (1.0 + preact * (1.0 - sigmoid)))


def project_kernel(features_hbm, weight_hbm, projected_ref, features, weight, sems):
    copies = [
        pltpu.make_async_copy(features_hbm, features, sems.at[0]),
        pltpu.make_async_copy(weight_hbm, weight, sems.at[1]),
    ]
    for copy in copies:
        copy.start()
    for copy in copies:
        copy.wait()
    projected_ref[...] = product(features[...], weight[...]).astype(BF)


def fill_kernel(blk_ref, live_ref, projected_ref, outgoing_hbm, zeros, sems):
    zeros[...] = jnp.zeros(zeros.shape, BF)
    parts = outgoing_hbm.shape[0]

    def start(part, carried):
        @pl.when(live_ref[part] > 0)
        def _():
            row = pl.multiple_of(blk_ref[part] * TILE, TILE)
            pltpu.make_async_copy(
                projected_ref.at[pl.ds(row, TILE)], outgoing_hbm.at[part], sems.at[part]
            ).start()

        @pl.when(live_ref[part] <= 0)
        def _():
            pltpu.make_async_copy(zeros, outgoing_hbm.at[part], sems.at[part]).start()

        return carried

    def wait(part, carried):
        pltpu.make_async_copy(zeros, outgoing_hbm.at[part], sems.at[part]).wait()
        return carried

    lax.fori_loop(0, parts, start, 0)
    lax.fori_loop(0, parts, wait, 0)


def spread_kernel(ring, blocks, pos_ref, count_ref, place_ref, tiles_ref, *outs):
    rows = blocks * TILE
    place = place_ref[0]
    for offset in range(ring):
        dense = outs[offset]
        dense[...] = jnp.zeros(dense.shape, BF)
        spot = lax.rem(place + offset, ring)
        for half in range(FAR):
            source = half * ring + spot

            def put(slot, carried, dense=dense, half=half, source=source):
                position = pos_ref[source * tiles_ref.shape[1] + slot]
                target = pl.multiple_of(position // blocks * TILE, TILE)
                origin = pl.multiple_of(half * rows + position % blocks * TILE, TILE)
                dense[pl.ds(target, TILE), pl.ds(origin, TILE)] = tiles_ref[source, slot]
                return carried

            lax.fori_loop(0, count_ref[source], put, 0)


def spread_cut_kernel(dst_ref, cut_ref, dense_hbm, dense, sem):
    chunks, _, columns = dense.shape
    chunk = columns // TILE
    dense[...] = jnp.zeros(dense.shape, BF)

    def put(part, carried):
        target = pl.multiple_of(dst_ref[part] * TILE, TILE)
        origin = pl.multiple_of(lax.rem(part, chunk) * TILE, TILE)
        dense[lax.div(part, chunk), pl.ds(target, TILE), pl.ds(origin, TILE)] = cut_ref[part]
        return carried

    lax.fori_loop(0, chunks * chunk, put, 0)
    copy = pltpu.make_async_copy(dense, dense_hbm, sem)
    copy.start()
    copy.wait()


def pair_kernel(half_ref, own_ref, other_ref, pair_ref):
    rows = own_ref.shape[0]
    place = pl.multiple_of(half_ref[0] * rows, TILE)
    pair_ref[pl.ds(place, rows)] = own_ref[...]
    pair_ref[pl.ds(pl.multiple_of(rows - place, TILE), rows)] = other_ref[...]


def middle_kernel(
    sum_hbm,
    cotangent_hbm,
    bias_ref,
    mat_hbm,
    cut_hbm,
    far_hbm,
    hidden_ref,
    grad_ref,
    low_ref,
    high_ref,
    terms_hbm,
    total,
    cotangent,
    mat,
    cut,
    far,
    terms,
    sems,
):
    rows, width = total.shape
    chunks = cut.shape[0]
    chunk = far.shape[0] // chunks
    move = lambda source, target, place: pltpu.make_async_copy(source, target, sems.at[place])
    copies = [move(sum_hbm, total, 2 * chunks)]
    for piece in range(chunks):
        span = pl.ds(piece * chunk, chunk)
        copies.append(move(cut_hbm.at[piece], cut.at[piece], piece))
        copies.append(move(far_hbm.at[span], far.at[span], chunks + piece))
    copies.append(move(cotangent_hbm, cotangent, 2 * chunks + 1))
    copies.append(move(mat_hbm, mat, 2 * chunks + 2))
    for copy in copies:
        copy.start()
    copies[0].wait()
    for piece in range(chunks):
        copies[1 + 2 * piece].wait()
        copies[2 + 2 * piece].wait()
        arrived = far[pl.ds(piece * chunk, chunk)].reshape(chunk * TILE, width)
        total[...] += product(cut[piece], arrived)
    activated, derivative = silu_parts(total[...] + bias_ref[...])
    hidden_ref[...] = activated.astype(BF)
    copies[-2].wait()
    grad = (cotangent[...].astype(F32) * derivative).T.astype(BF)
    grad_ref[...] = grad
    copies[-1].wait()
    low_ref[...] = product(grad, mat[:, :rows]).astype(BF)
    high_ref[...] = product(grad, mat[:, rows:]).astype(BF)
    stores = []
    for piece in range(chunks):
        result = product(grad, cut[piece]).astype(BF)
        for slot in range(chunk):
            terms[piece * chunk + slot] = result[:, slot * TILE : (slot + 1) * TILE]
        span = pl.ds(piece * chunk, chunk)
        stores.append(move(terms.at[span], terms_hbm.at[span], 2 * chunks + 3 + piece))
        stores[-1].start()
    for copy in stores:
        copy.wait()


def gather_kernel(blk_ref, live_ref, arrived_ref, total_ref):
    total_ref[...] = jnp.zeros(total_ref.shape, F32)

    def add(part, carried):
        @pl.when(live_ref[part] > 0)
        def _():
            columns = pl.ds(pl.multiple_of(blk_ref[part] * TILE, TILE), TILE)
            total_ref[:, columns] += arrived_ref[part].astype(F32)

        return carried

    lax.fori_loop(0, arrived_ref.shape[0], add, 0)


def hop_kernel(at, grad_ref, mat_ref, arrived_ref, out_ref):
    wide, held = out_ref.shape[1], arrived_ref.shape[1]
    for low, high in ((0, at), (at, at + held), (at + held, wide)):
        if low < high:
            term = product(grad_ref[...], mat_ref[:, low:high])
            if low == at:
                term += arrived_ref[...].astype(F32)
            out_ref[:, low:high] = term.astype(BF)


def close_kernel(half_ref, grad_ref, mat_ref, left_ref, right_ref, own_ref, other_ref):
    rows = grad_ref.shape[1]
    mine = pl.ds(pl.multiple_of(half_ref[0] * rows, TILE), rows)
    theirs = pl.ds(pl.multiple_of((1 - half_ref[0]) * rows, TILE), rows)

    def total(columns):
        arrived = left_ref[:, columns].astype(F32) + right_ref[:, columns].astype(F32)
        return product(grad_ref[...], mat_ref[:, columns]) + arrived

    other_ref[...] = total(theirs).astype(BF)
    own_ref[...] = total(mine)


def last_kernel(own_ref, other_ref, cut_ref, weight_ref, out_ref):
    total = own_ref[...] + other_ref[...].astype(F32) + cut_ref[...]
    out_ref[...] = lax.dot_general(
        total.T.astype(BF), weight_ref[...], (((1,), (1,)), ((), ())), preferred_element_type=F32
    ).astype(BF)


def on_device(
    features,
    weight,
    bias,
    cotangent,
    in_tiles,
    in_pos,
    in_count,
    cut_tiles,
    send_blk,
    send_live,
    recv_dst,
):
    rows, width = features.shape
    blocks = rows // TILE
    peers = lax.axis_size("blk")
    parts = lax.axis_size("dom")
    ring = peers // FAR
    reach = ring // 2
    me = lax.axis_index("blk")
    place, half = me % ring, me // ring
    wide = FAR * rows
    send_to, is_live, dst = send_blk[0, 0], send_live[0, 0], recv_dst[0, 0]
    shape = jax.ShapeDtypeStruct

    def along_ring(value, by):
        moves = [
            (side * ring + spot, side * ring + (spot + by) % ring)
            for side in range(FAR)
            for spot in range(ring)
        ]
        return lax.ppermute(value, "blk", moves)

    def across(value):
        return lax.ppermute(value, "blk", [(i, (i + ring) % peers) for i in range(peers)])

    projected = call(
        project_kernel,
        "project",
        shape((rows, width), BF),
        [HBM, HBM],
        VMEM,
        [
            pltpu.VMEM(features.shape, BF),
            pltpu.VMEM(weight.shape, BF),
            pltpu.SemaphoreType.DMA((2,)),
        ],
    )(in_hbm(features), in_hbm(weight))
    partner = across(projected)
    outgoing = call(
        fill_kernel,
        "fill",
        pltpu.HBM((parts, TILE, width), BF),
        [SMEM, SMEM, VMEM],
        HBM,
        [pltpu.VMEM((TILE, width), BF), pltpu.SemaphoreType.DMA((parts,))],
    )(send_to, is_live, projected)
    incoming = lax.all_to_all(outgoing, "dom", split_axis=0, concat_axis=0, tiled=True)

    dense = call(
        lambda *refs: spread_kernel(ring, blocks, *refs),
        "spread",
        tuple([shape((rows, wide), BF)] * ring),
        [SMEM, SMEM, SMEM, VMEM],
        tuple([VMEM] * ring),
        moved=10 << 20,
    )(in_pos[0, 0].reshape(-1), in_count[0, 0], place.reshape(1), in_tiles[0, 0])
    dense_cut = call(
        spread_cut_kernel,
        "spread_cut",
        pltpu.HBM((CHUNKS, rows, parts // CHUNKS * TILE), BF),
        [SMEM, VMEM],
        HBM,
        [
            pltpu.VMEM((CHUNKS, rows, parts // CHUNKS * TILE), BF),
            pltpu.SemaphoreType.DMA,
        ],
        moved=6 << 20,
    )(dst, cut_tiles[0, 0])

    pair = call(
        pair_kernel, "pair", shape((wide, width), BF), [SMEM, VMEM, VMEM], VMEM, flops=PAIR_COST
    )(half.reshape(1), projected, partner)
    running = product(dense[0], pair)
    right = left = pair
    for hop in range(1, reach):
        right, left = along_ring(right, 1), along_ring(left, -1)
        running = running + product(dense[ring - hop], right)
        running = running + product(dense[hop], left)
    low, high = along_ring(right[:rows], 1), along_ring(left[rows:], -1)

    running = running + product(dense[reach][:, :rows], low)
    running = running + product(dense[reach][:, rows:], high)

    hidden, grad_pre, low, high, terms = call(
        middle_kernel,
        "middle",
        (shape((rows, width), BF),)
        + (shape((width, rows), BF),) * 3
        + (pltpu.HBM((parts, width, TILE), BF),),
        [HBM, HBM, VMEM, HBM, HBM, HBM],
        (VMEM,) * 4 + (HBM,),
        [
            pltpu.VMEM((rows, width), F32),
            pltpu.VMEM((rows, width), BF),
            pltpu.VMEM((rows, wide), BF),
            pltpu.VMEM(dense_cut.shape, BF),
            pltpu.VMEM((parts, TILE, width), BF),
            pltpu.VMEM((parts, width, TILE), BF),
            pltpu.SemaphoreType.DMA((3 * CHUNKS + 3,)),
        ],
    )(
        in_hbm(running),
        in_hbm(cotangent),
        bias.reshape(1, width),
        in_hbm(dense[reach]),
        in_hbm(dense_cut),
        in_hbm(incoming),
    )

    def add_on(mat, arrived, at):
        return call(
            lambda *refs: hop_kernel(at, *refs), "hop", shape((width, wide), BF), [VMEM] * 3, VMEM
        )(grad_pre, mat, arrived)

    low, high = along_ring(low, 1), along_ring(high, -1)
    returned = lax.all_to_all(terms, "dom", split_axis=0, concat_axis=0, tiled=True)
    for hop in range(reach - 1, 0, -1):
        first = hop == reach - 1
        right = add_on(dense[hop], low if first else from_left, 0)
        left = add_on(dense[ring - hop], high if first else from_right, rows if first else 0)
        from_left, from_right = along_ring(right, 1), along_ring(left, -1)
    own, other = call(
        close_kernel,
        "close",
        (shape((width, rows), F32), shape((width, rows), BF)),
        [SMEM] + [VMEM] * 4,
        (VMEM, VMEM),
        flops=CLOSE_COST,
    )(half.reshape(1), grad_pre, dense[0], from_left, from_right)
    other = across(other)
    from_cuts = call(
        gather_kernel, "gather", shape((width, rows), F32), [SMEM, SMEM, VMEM], VMEM, moved=2 << 20
    )(send_to, is_live, returned)
    grad_features = call(
        last_kernel, "last", shape((rows, width), BF), [VMEM] * 4, VMEM
    )(own, other, from_cuts, weight)
    return (hidden, grad_features)


def solution(mesh):
    in_specs = (
        P(("dom", "blk"), None),
        P(),
        P(),
        P(("dom", "blk"), None),
        P("dom", "blk", None, None, None, None),
        P("dom", "blk", None, None),
        P("dom", "blk", None),
        P("dom", "blk", None, None, None),
        P("dom", "blk", None),
        P("dom", "blk", None),
        P("dom", "blk", None),
    )
    out_specs = (P(("dom", "blk"), None), P(("dom", "blk"), None))
    return jax.shard_map(
        on_device, mesh=mesh, in_specs=in_specs, out_specs=out_specs, check_vma=False
    )
```

```python
import jax
import jax.numpy as jnp
from jax import lax
from jax.experimental import pallas as pl
from jax.experimental.pallas import tpu as pltpu
from jax.sharding import PartitionSpec as P

BF, F32 = jnp.bfloat16, jnp.float32
TILE = 128
FAR = 2
CHUNKS = 4
VMEM_LIMIT = 16 * 1024 * 1024
PAIR_COST = 100_000_000_000
TERMS_COST = 1_600_000_000
CLOSE_COST = 30_500_000_000


def spec(space):
    return pl.BlockSpec(memory_space=space)


SMEM, VMEM, HBM = spec(pltpu.SMEM), spec(pltpu.VMEM), spec(pltpu.HBM)


def call(kernel, name, out_shape, in_specs, out_specs, scratch=(), flops=0, moved=0):
    return pl.pallas_call(
        kernel,
        out_shape=out_shape,
        in_specs=in_specs,
        out_specs=out_specs,
        scratch_shapes=scratch,
        compiler_params=pltpu.CompilerParams(vmem_limit_bytes=VMEM_LIMIT),
        cost_estimate=pl.CostEstimate(flops=flops, bytes_accessed=moved, transcendentals=0),
        name=name,
    )


def in_hbm(value):
    return pltpu.with_memory_space_constraint(value, pltpu.HBM)


def product(left, right):
    return jnp.dot(left, right, preferred_element_type=F32)


def silu_parts(preact):
    sigmoid = 1.0 / (1.0 + jnp.exp(-preact))
    return (preact * sigmoid, sigmoid * (1.0 + preact * (1.0 - sigmoid)))


def project_kernel(features_hbm, weight_hbm, projected_ref, features, weight, sems):
    copies = [
        pltpu.make_async_copy(features_hbm, features, sems.at[0]),
        pltpu.make_async_copy(weight_hbm, weight, sems.at[1]),
    ]
    for copy in copies:
        copy.start()
    for copy in copies:
        copy.wait()
    projected_ref[...] = product(features[...], weight[...]).astype(BF)


def fill_kernel(blk_ref, live_ref, projected_ref, outgoing_hbm, zeros, sems):
    zeros[...] = jnp.zeros(zeros.shape, BF)
    parts = outgoing_hbm.shape[0]

    def start(part, carried):
        @pl.when(live_ref[part] > 0)
        def _():
            row = pl.multiple_of(blk_ref[part] * TILE, TILE)
            pltpu.make_async_copy(
                projected_ref.at[pl.ds(row, TILE)], outgoing_hbm.at[part], sems.at[part]
            ).start()

        @pl.when(live_ref[part] <= 0)
        def _():
            pltpu.make_async_copy(zeros, outgoing_hbm.at[part], sems.at[part]).start()

        return carried

    def wait(part, carried):
        pltpu.make_async_copy(zeros, outgoing_hbm.at[part], sems.at[part]).wait()
        return carried

    lax.fori_loop(0, parts, start, 0)
    lax.fori_loop(0, parts, wait, 0)


def spread_kernel(ring, blocks, pos_ref, count_ref, place_ref, tiles_ref, *outs):
    rows = blocks * TILE
    place = place_ref[0]
    for offset in range(ring):
        dense = outs[offset]
        dense[...] = jnp.zeros(dense.shape, BF)
        spot = lax.rem(place + offset, ring)
        for half in range(FAR):
            source = half * ring + spot

            def put(slot, carried, dense=dense, half=half, source=source):
                position = pos_ref[source * tiles_ref.shape[1] + slot]
                target = pl.multiple_of(position // blocks * TILE, TILE)
                origin = pl.multiple_of(half * rows + position % blocks * TILE, TILE)
                dense[pl.ds(target, TILE), pl.ds(origin, TILE)] = tiles_ref[source, slot]
                return carried

            lax.fori_loop(0, count_ref[source], put, 0)


def spread_cut_kernel(dst_ref, cut_ref, dense_hbm, dense, sem):
    chunks, _, columns = dense.shape
    chunk = columns // TILE
    dense[...] = jnp.zeros(dense.shape, BF)

    def put(part, carried):
        target = pl.multiple_of(dst_ref[part] * TILE, TILE)
        origin = pl.multiple_of(lax.rem(part, chunk) * TILE, TILE)
        dense[lax.div(part, chunk), pl.ds(target, TILE), pl.ds(origin, TILE)] = cut_ref[part]
        return carried

    lax.fori_loop(0, chunks * chunk, put, 0)
    copy = pltpu.make_async_copy(dense, dense_hbm, sem)
    copy.start()
    copy.wait()


def pair_kernel(half_ref, own_ref, other_ref, pair_ref):
    rows = own_ref.shape[0]
    place = pl.multiple_of(half_ref[0] * rows, TILE)
    pair_ref[pl.ds(place, rows)] = own_ref[...]
    pair_ref[pl.ds(pl.multiple_of(rows - place, TILE), rows)] = other_ref[...]


def tail_kernel(sum_ref, mat_a, from_a, mat_b, from_b, mat_c, from_c, out_hbm, total, sem):
    total[...] = (
        sum_ref[...]
        + product(mat_a[...], from_a[...])
        + product(mat_b[...], from_b[...])
        + product(mat_c[...], from_c[...])
    )
    copy = pltpu.make_async_copy(total, out_hbm, sem)
    copy.start()
    copy.wait()


def middle_kernel(
    sum_hbm,
    cotangent_hbm,
    bias_ref,
    right_hbm,
    left_hbm,
    across_hbm,
    cut_hbm,
    far_hbm,
    hidden_ref,
    grad_ref,
    right_ref,
    left_ref,
    across_ref,
    total,
    cotangent,
    mats,
    cut,
    far,
    sems,
):
    rows, width = total.shape
    chunks = cut.shape[0]
    chunk = far.shape[0] // chunks
    move = lambda source, target, place: pltpu.make_async_copy(source, target, sems.at[place])
    copies = [move(sum_hbm, total, 2 * chunks)]
    for piece in range(chunks):
        span = pl.ds(piece * chunk, chunk)
        copies.append(move(cut_hbm.at[piece], cut.at[piece], piece))
        copies.append(move(far_hbm.at[span], far.at[span], chunks + piece))
    copies.append(move(cotangent_hbm, cotangent, 2 * chunks + 1))
    for place, mat in enumerate((right_hbm, left_hbm, across_hbm)):
        copies.append(move(mat, mats.at[place], 2 * chunks + 2 + place))
    for copy in copies:
        copy.start()
    copies[0].wait()
    for piece in range(chunks):
        copies[1 + 2 * piece].wait()
        copies[2 + 2 * piece].wait()
        arrived = far[pl.ds(piece * chunk, chunk)].reshape(chunk * TILE, width)
        total[...] += product(cut[piece], arrived)
    activated, derivative = silu_parts(total[...] + bias_ref[...])
    hidden_ref[...] = activated.astype(BF)
    copies[-4].wait()
    grad = (cotangent[...].astype(F32) * derivative).T.astype(BF)
    grad_ref[...] = grad
    for place, out_ref in enumerate((right_ref, left_ref, across_ref)):
        copies[place - 3].wait()
        out_ref[...] = product(grad, mats[place]).astype(BF)


def terms_kernel(grad_ref, cut_hbm, terms_hbm, cut, terms, sems):
    chunks = cut.shape[0]
    chunk = terms.shape[0] // chunks
    loads = [
        pltpu.make_async_copy(cut_hbm.at[piece], cut.at[piece], sems.at[piece])
        for piece in range(chunks)
    ]
    stores = []
    for copy in loads:
        copy.start()
    for piece in range(chunks):
        loads[piece].wait()
        result = product(grad_ref[...], cut[piece]).astype(BF)
        for slot in range(chunk):
            terms[piece * chunk + slot] = result[:, slot * TILE : (slot + 1) * TILE]
        span = pl.ds(piece * chunk, chunk)
        stores.append(
            pltpu.make_async_copy(terms.at[span], terms_hbm.at[span], sems.at[chunks + piece])
        )
        stores[-1].start()
    for copy in stores:
        copy.wait()


def gather_kernel(blk_ref, live_ref, arrived_ref, total_ref):
    total_ref[...] = jnp.zeros(total_ref.shape, F32)

    def add(part, carried):
        @pl.when(live_ref[part] > 0)
        def _():
            columns = pl.ds(pl.multiple_of(blk_ref[part] * TILE, TILE), TILE)
            total_ref[:, columns] += arrived_ref[part].astype(F32)

        return carried

    lax.fori_loop(0, arrived_ref.shape[0], add, 0)


def hop_kernel(grad_ref, mat_ref, arrived_ref, out_ref):
    term = product(grad_ref[...], mat_ref[...]) + arrived_ref[...].astype(F32)
    out_ref[...] = term.astype(BF)


def close_kernel(
    half_ref, grad_ref, mat_ref, left_ref, right_ref, across_ref, own_ref, other_ref
):
    rows = grad_ref.shape[1]
    mine = pl.ds(pl.multiple_of(half_ref[0] * rows, TILE), rows)
    theirs = pl.ds(pl.multiple_of((1 - half_ref[0]) * rows, TILE), rows)

    def total(columns):
        arrived = left_ref[:, columns].astype(F32) + right_ref[:, columns].astype(F32)
        arrived += across_ref[:, columns].astype(F32)
        return product(grad_ref[...], mat_ref[:, columns]) + arrived

    other_ref[...] = total(theirs).astype(BF)
    own_ref[...] = total(mine)


def last_kernel(own_ref, other_ref, cut_ref, weight_ref, out_ref):
    total = own_ref[...] + other_ref[...].astype(F32) + cut_ref[...]
    out_ref[...] = lax.dot_general(
        total.T.astype(BF), weight_ref[...], (((1,), (1,)), ((), ())), preferred_element_type=F32
    ).astype(BF)


def on_device(
    features,
    weight,
    bias,
    cotangent,
    in_tiles,
    in_pos,
    in_count,
    cut_tiles,
    send_blk,
    send_live,
    recv_dst,
):
    rows, width = features.shape
    blocks = rows // TILE
    peers = lax.axis_size("blk")
    parts = lax.axis_size("dom")
    ring = peers // FAR
    reach = ring // 2
    me = lax.axis_index("blk")
    place, half = me % ring, me // ring
    wide = FAR * rows
    send_to, is_live, dst = send_blk[0, 0], send_live[0, 0], recv_dst[0, 0]
    shape = jax.ShapeDtypeStruct

    def along_ring(value, by):
        moves = [
            (side * ring + spot, side * ring + (spot + by) % ring)
            for side in range(FAR)
            for spot in range(ring)
        ]
        return lax.ppermute(value, "blk", moves)

    def across(value):
        return lax.ppermute(value, "blk", [(i, (i + ring) % peers) for i in range(peers)])

    projected = call(
        project_kernel,
        "project",
        shape((rows, width), BF),
        [HBM, HBM],
        VMEM,
        [
            pltpu.VMEM(features.shape, BF),
            pltpu.VMEM(weight.shape, BF),
            pltpu.SemaphoreType.DMA((2,)),
        ],
    )(in_hbm(features), in_hbm(weight))
    partner = across(projected)
    outgoing = call(
        fill_kernel,
        "fill",
        pltpu.HBM((parts, TILE, width), BF),
        [SMEM, SMEM, VMEM],
        HBM,
        [pltpu.VMEM((TILE, width), BF), pltpu.SemaphoreType.DMA((parts,))],
    )(send_to, is_live, projected)
    incoming = lax.all_to_all(outgoing, "dom", split_axis=0, concat_axis=0, tiled=True)

    dense = call(
        lambda *refs: spread_kernel(ring, blocks, *refs),
        "spread",
        tuple([shape((rows, wide), BF)] * ring),
        [SMEM, SMEM, SMEM, VMEM],
        tuple([VMEM] * ring),
        moved=10 << 20,
    )(in_pos[0, 0].reshape(-1), in_count[0, 0], place.reshape(1), in_tiles[0, 0])
    dense_cut = call(
        spread_cut_kernel,
        "spread_cut",
        pltpu.HBM((CHUNKS, rows, parts // CHUNKS * TILE), BF),
        [SMEM, VMEM],
        HBM,
        [
            pltpu.VMEM((CHUNKS, rows, parts // CHUNKS * TILE), BF),
            pltpu.SemaphoreType.DMA,
        ],
        moved=6 << 20,
    )(dst, cut_tiles[0, 0])

    pair = call(
        pair_kernel, "pair", shape((wide, width), BF), [SMEM, VMEM, VMEM], VMEM, flops=PAIR_COST
    )(half.reshape(1), projected, partner)
    running = product(dense[0], pair)
    right = left = pair
    across_ring = along_ring(pair, reach)
    for hop in range(1, reach):
        right, left = along_ring(right, 1), along_ring(left, -1)
        if hop < reach - 1:
            running = running + product(dense[ring - hop], right)
            running = running + product(dense[hop], left)
    running = call(
        tail_kernel,
        "tail",
        pltpu.HBM((rows, width), F32),
        [VMEM] * 7,
        HBM,
        [pltpu.VMEM((rows, width), F32), pltpu.SemaphoreType.DMA],
    )(running, dense[reach + 1], right, dense[reach - 1], left, dense[reach], across_ring)

    hidden, grad_pre, right, left, across_ring = call(
        middle_kernel,
        "middle",
        (shape((rows, width), BF), shape((width, rows), BF)) + (shape((width, wide), BF),) * 3,
        [HBM, HBM, VMEM] + [HBM] * 5,
        (VMEM,) * 5,
        [
            pltpu.VMEM((rows, width), F32),
            pltpu.VMEM((rows, width), BF),
            pltpu.VMEM((3, rows, wide), BF),
            pltpu.VMEM(dense_cut.shape, BF),
            pltpu.VMEM((parts, TILE, width), BF),
            pltpu.SemaphoreType.DMA((2 * CHUNKS + 5,)),
        ],
    )(
        in_hbm(running),
        in_hbm(cotangent),
        bias.reshape(1, width),
        in_hbm(dense[reach - 1]),
        in_hbm(dense[reach + 1]),
        in_hbm(dense[reach]),
        in_hbm(dense_cut),
        in_hbm(incoming),
    )

    def add_on(mat, arrived):
        return call(hop_kernel, "hop", shape((width, wide), BF), [VMEM] * 3, VMEM)(
            grad_pre, mat, arrived
        )

    right, left = along_ring(right, 1), along_ring(left, -1)
    across_ring = along_ring(across_ring, reach)
    terms = call(
        terms_kernel,
        "terms",
        pltpu.HBM((parts, width, TILE), BF),
        [VMEM, HBM],
        HBM,
        [
            pltpu.VMEM(dense_cut.shape, BF),
            pltpu.VMEM((parts, width, TILE), BF),
            pltpu.SemaphoreType.DMA((2 * CHUNKS,)),
        ],
        flops=TERMS_COST,
    )(grad_pre, in_hbm(dense_cut))
    returned = lax.all_to_all(terms, "dom", split_axis=0, concat_axis=0, tiled=True)
    for hop in range(reach - 2, 0, -1):
        right = along_ring(add_on(dense[hop], right), 1)
        left = along_ring(add_on(dense[ring - hop], left), -1)
    own, other = call(
        close_kernel,
        "close",
        (shape((width, rows), F32), shape((width, rows), BF)),
        [SMEM] + [VMEM] * 5,
        (VMEM, VMEM),
        flops=CLOSE_COST,
    )(half.reshape(1), grad_pre, dense[0], right, left, across_ring)
    other = across(other)
    from_cuts = call(
        gather_kernel, "gather", shape((width, rows), F32), [SMEM, SMEM, VMEM], VMEM, moved=2 << 20
    )(send_to, is_live, returned)
    grad_features = call(
        last_kernel, "last", shape((rows, width), BF), [VMEM] * 4, VMEM
    )(own, other, from_cuts, weight)
    return (hidden, grad_features)


def solution(mesh):
    in_specs = (
        P(("dom", "blk"), None),
        P(),
        P(),
        P(("dom", "blk"), None),
        P("dom", "blk", None, None, None, None),
        P("dom", "blk", None, None),
        P("dom", "blk", None),
        P("dom", "blk", None, None, None),
        P("dom", "blk", None),
        P("dom", "blk", None),
        P("dom", "blk", None),
    )
    out_specs = (P(("dom", "blk"), None), P(("dom", "blk"), None))
    return jax.shard_map(
        on_device, mesh=mesh, in_specs=in_specs, out_specs=out_specs, check_vma=False
    )
```

```python
import jax
import jax.numpy as jnp
from jax import lax
from jax.experimental import pallas as pl
from jax.experimental.pallas import tpu as pltpu
from jax.sharding import PartitionSpec as P

BF, F32 = jnp.bfloat16, jnp.float32
TILE = 128
FAR = 2
CHUNKS = 4
VMEM_LIMIT = 16 * 1024 * 1024
PAIR_COST = 100_000_000_000
CLOSE_COST = 26_500_000_000
CUT_COST = 2_000_000_000


def spec(space):
    return pl.BlockSpec(memory_space=space)


SMEM, VMEM, HBM = spec(pltpu.SMEM), spec(pltpu.VMEM), spec(pltpu.HBM)


def call(kernel, name, out_shape, in_specs, out_specs, scratch=(), flops=0, moved=0):
    return pl.pallas_call(
        kernel,
        out_shape=out_shape,
        in_specs=in_specs,
        out_specs=out_specs,
        scratch_shapes=scratch,
        compiler_params=pltpu.CompilerParams(vmem_limit_bytes=VMEM_LIMIT),
        cost_estimate=pl.CostEstimate(flops=flops, bytes_accessed=moved, transcendentals=0),
        name=name,
    )


def in_hbm(value):
    return pltpu.with_memory_space_constraint(value, pltpu.HBM)


def product(left, right):
    return jnp.dot(left, right, preferred_element_type=F32)


def silu_parts(preact):
    sigmoid = 1.0 / (1.0 + jnp.exp(-preact))
    return (preact * sigmoid, sigmoid * (1.0 + preact * (1.0 - sigmoid)))


def project_kernel(features_hbm, weight_hbm, projected_ref, features, weight, sems):
    copies = [
        pltpu.make_async_copy(features_hbm, features, sems.at[0]),
        pltpu.make_async_copy(weight_hbm, weight, sems.at[1]),
    ]
    for copy in copies:
        copy.start()
    for copy in copies:
        copy.wait()
    projected_ref[...] = product(features[...], weight[...]).astype(BF)


def fill_kernel(blk_ref, live_ref, projected_ref, outgoing_hbm, zeros, sems):
    zeros[...] = jnp.zeros(zeros.shape, BF)
    parts = outgoing_hbm.shape[0]

    def start(part, carried):
        @pl.when(live_ref[part] > 0)
        def _():
            row = pl.multiple_of(blk_ref[part] * TILE, TILE)
            pltpu.make_async_copy(
                projected_ref.at[pl.ds(row, TILE)], outgoing_hbm.at[part], sems.at[part]
            ).start()

        @pl.when(live_ref[part] <= 0)
        def _():
            pltpu.make_async_copy(zeros, outgoing_hbm.at[part], sems.at[part]).start()

        return carried

    def wait(part, carried):
        pltpu.make_async_copy(zeros, outgoing_hbm.at[part], sems.at[part]).wait()
        return carried

    lax.fori_loop(0, parts, start, 0)
    lax.fori_loop(0, parts, wait, 0)


def spread_kernel(ring, blocks, pos_ref, count_ref, place_ref, tiles_ref, *outs):
    rows = blocks * TILE
    place = place_ref[0]
    for offset in range(ring):
        dense = outs[offset]
        dense[...] = jnp.zeros(dense.shape, BF)
        spot = lax.rem(place + offset, ring)
        for half in range(FAR):
            source = half * ring + spot

            def put(slot, carried, dense=dense, half=half, source=source):
                position = pos_ref[source * tiles_ref.shape[1] + slot]
                target = pl.multiple_of(position // blocks * TILE, TILE)
                origin = pl.multiple_of(half * rows + position % blocks * TILE, TILE)
                dense[pl.ds(target, TILE), pl.ds(origin, TILE)] = tiles_ref[source, slot]
                return carried

            lax.fori_loop(0, count_ref[source], put, 0)


def spread_cut_kernel(dst_ref, cut_ref, dense_hbm, dense, sem):
    chunks, _, columns = dense.shape
    chunk = columns // TILE
    dense[...] = jnp.zeros(dense.shape, BF)

    def put(part, carried):
        target = pl.multiple_of(dst_ref[part] * TILE, TILE)
        origin = pl.multiple_of(lax.rem(part, chunk) * TILE, TILE)
        dense[lax.div(part, chunk), pl.ds(target, TILE), pl.ds(origin, TILE)] = cut_ref[part]
        return carried

    lax.fori_loop(0, chunks * chunk, put, 0)
    copy = pltpu.make_async_copy(dense, dense_hbm, sem)
    copy.start()
    copy.wait()


def pair_kernel(half_ref, own_ref, other_ref, pair_ref):
    rows = own_ref.shape[0]
    place = pl.multiple_of(half_ref[0] * rows, TILE)
    pair_ref[pl.ds(place, rows)] = own_ref[...]
    pair_ref[pl.ds(pl.multiple_of(rows - place, TILE), rows)] = other_ref[...]


def cut_sum_kernel(cut_hbm, far_hbm, total_ref, cut, far, sems):
    chunks = cut.shape[0]
    chunk = far.shape[0] // chunks
    width = far.shape[2]
    copies = []
    for piece in range(chunks):
        span = pl.ds(piece * chunk, chunk)
        copies.append(
            (
                pltpu.make_async_copy(cut_hbm.at[piece], cut.at[piece], sems.at[piece]),
                pltpu.make_async_copy(far_hbm.at[span], far.at[span], sems.at[chunks + piece]),
            )
        )
    for pair in copies:
        for copy in pair:
            copy.start()
    for piece in range(chunks):
        for copy in copies[piece]:
            copy.wait()
        arrived = far[pl.ds(piece * chunk, chunk)].reshape(chunk * TILE, width)
        term = product(cut[piece], arrived)
        total_ref[...] = term if piece == 0 else total_ref[...] + term


def middle_kernel(
    sum_ref,
    cut_sum_ref,
    last_ref,
    bias_ref,
    cotangent_ref,
    far_mat_ref,
    near_mat_ref,
    cut_hbm,
    hidden_ref,
    grad_ref,
    left_ref,
    right_ref,
    terms_hbm,
    cut,
    terms,
    sems,
):
    chunks = cut.shape[0]
    chunk = terms.shape[0] // chunks
    loads = [
        pltpu.make_async_copy(cut_hbm.at[piece], cut.at[piece], sems.at[piece])
        for piece in range(chunks)
    ]
    for copy in loads:
        copy.start()
    total = sum_ref[...] + cut_sum_ref[...] + product(far_mat_ref[...], last_ref[...])
    activated, derivative = silu_parts(total + bias_ref[...])
    hidden_ref[...] = activated.astype(BF)
    grad = (cotangent_ref[...].astype(F32) * derivative).T.astype(BF)
    grad_ref[...] = grad
    left_ref[...] = product(grad, far_mat_ref[...]).astype(BF)
    right_ref[...] = product(grad, near_mat_ref[...]).astype(BF)
    stores = []
    for piece in range(chunks):
        loads[piece].wait()
        result = product(grad, cut[piece]).astype(BF)
        for slot in range(chunk):
            terms[piece * chunk + slot] = result[:, slot * TILE : (slot + 1) * TILE]
        span = pl.ds(piece * chunk, chunk)
        stores.append(
            pltpu.make_async_copy(terms.at[span], terms_hbm.at[span], sems.at[chunks + piece])
        )
        stores[-1].start()
    for copy in stores:
        copy.wait()


def gather_kernel(blk_ref, live_ref, arrived_ref, total_ref):
    total_ref[...] = jnp.zeros(total_ref.shape, F32)

    def add(part, carried):
        @pl.when(live_ref[part] > 0)
        def _():
            columns = pl.ds(pl.multiple_of(blk_ref[part] * TILE, TILE), TILE)
            total_ref[:, columns] += arrived_ref[part].astype(F32)

        return carried

    lax.fori_loop(0, arrived_ref.shape[0], add, 0)


def hop_kernel(grad_ref, mat_ref, arrived_ref, out_ref):
    term = product(grad_ref[...], mat_ref[...]) + arrived_ref[...].astype(F32)
    out_ref[...] = term.astype(BF)


def close_kernel(half_ref, grad_ref, mat_ref, left_ref, right_ref, own_ref, other_ref):
    rows = grad_ref.shape[1]
    mine = pl.ds(pl.multiple_of(half_ref[0] * rows, TILE), rows)
    theirs = pl.ds(pl.multiple_of((1 - half_ref[0]) * rows, TILE), rows)

    def total(columns):
        arrived = left_ref[:, columns].astype(F32) + right_ref[:, columns].astype(F32)
        return product(grad_ref[...], mat_ref[:, columns]) + arrived

    other_ref[...] = total(theirs).astype(BF)
    own_ref[...] = total(mine)


def last_kernel(own_ref, other_ref, cut_ref, weight_ref, out_ref):
    total = own_ref[...] + other_ref[...].astype(F32) + cut_ref[...]
    out_ref[...] = lax.dot_general(
        total.T.astype(BF), weight_ref[...], (((1,), (1,)), ((), ())), preferred_element_type=F32
    ).astype(BF)


def on_device(
    features,
    weight,
    bias,
    cotangent,
    in_tiles,
    in_pos,
    in_count,
    cut_tiles,
    send_blk,
    send_live,
    recv_dst,
):
    rows, width = features.shape
    blocks = rows // TILE
    peers = lax.axis_size("blk")
    parts = lax.axis_size("dom")
    ring = peers // FAR
    reach = ring // 2
    me = lax.axis_index("blk")
    place, half = me % ring, me // ring
    wide = FAR * rows
    send_to, is_live, dst = send_blk[0, 0], send_live[0, 0], recv_dst[0, 0]
    shape = jax.ShapeDtypeStruct

    def along_ring(value, by):
        moves = [
            (side * ring + spot, side * ring + (spot + by) % ring)
            for side in range(FAR)
            for spot in range(ring)
        ]
        return lax.ppermute(value, "blk", moves)

    def across(value):
        return lax.ppermute(value, "blk", [(i, (i + ring) % peers) for i in range(peers)])

    projected = call(
        project_kernel,
        "project",
        shape((rows, width), BF),
        [HBM, HBM],
        VMEM,
        [
            pltpu.VMEM(features.shape, BF),
            pltpu.VMEM(weight.shape, BF),
            pltpu.SemaphoreType.DMA((2,)),
        ],
    )(in_hbm(features), in_hbm(weight))
    partner = across(projected)
    outgoing = call(
        fill_kernel,
        "fill",
        pltpu.HBM((parts, TILE, width), BF),
        [SMEM, SMEM, VMEM],
        HBM,
        [pltpu.VMEM((TILE, width), BF), pltpu.SemaphoreType.DMA((parts,))],
    )(send_to, is_live, projected)
    incoming = lax.all_to_all(outgoing, "dom", split_axis=0, concat_axis=0, tiled=True)

    dense = call(
        lambda *refs: spread_kernel(ring, blocks, *refs),
        "spread",
        tuple([shape((rows, wide), BF)] * ring),
        [SMEM, SMEM, SMEM, VMEM],
        tuple([VMEM] * ring),
        moved=10 << 20,
    )(in_pos[0, 0].reshape(-1), in_count[0, 0], place.reshape(1), in_tiles[0, 0])
    dense_cut = call(
        spread_cut_kernel,
        "spread_cut",
        pltpu.HBM((CHUNKS, rows, parts // CHUNKS * TILE), BF),
        [SMEM, VMEM],
        HBM,
        [
            pltpu.VMEM((CHUNKS, rows, parts // CHUNKS * TILE), BF),
            pltpu.SemaphoreType.DMA,
        ],
        moved=6 << 20,
    )(dst, cut_tiles[0, 0])

    pair = call(
        pair_kernel, "pair", shape((wide, width), BF), [SMEM, VMEM, VMEM], VMEM, flops=PAIR_COST
    )(half.reshape(1), projected, partner)
    running = product(dense[0], pair)
    right = left = pair
    for hop in range(1, reach):
        left, right = along_ring(left, -1), along_ring(right, 1)
        running = running + product(dense[hop], left)
        running = running + product(dense[ring - hop], right)
    left = along_ring(left, -1)
    cut_sum = call(
        cut_sum_kernel,
        "cut_sum",
        shape((rows, width), F32),
        [HBM, HBM],
        VMEM,
        [
            pltpu.VMEM(dense_cut.shape, BF),
            pltpu.VMEM((parts, TILE, width), BF),
            pltpu.SemaphoreType.DMA((2 * CHUNKS,)),
        ],
        flops=CUT_COST,
    )(in_hbm(dense_cut), in_hbm(incoming))

    hidden, grad_pre, left, right, terms = call(
        middle_kernel,
        "middle",
        (shape((rows, width), BF), shape((width, rows), BF))
        + (shape((width, wide), BF),) * 2
        + (pltpu.HBM((parts, width, TILE), BF),),
        [VMEM] * 7 + [HBM],
        (VMEM,) * 4 + (HBM,),
        [
            pltpu.VMEM(dense_cut.shape, BF),
            pltpu.VMEM((parts, width, TILE), BF),
            pltpu.SemaphoreType.DMA((2 * CHUNKS,)),
        ],
    )(
        running,
        cut_sum,
        left,
        bias.reshape(1, width),
        cotangent,
        dense[reach],
        dense[reach - 1],
        in_hbm(dense_cut),
    )

    def add_on(mat, arrived):
        return call(hop_kernel, "hop", shape((width, wide), BF), [VMEM] * 3, VMEM)(
            grad_pre, mat, arrived
        )

    left, right = along_ring(left, -1), along_ring(right, 1)
    returned = lax.all_to_all(terms, "dom", split_axis=0, concat_axis=0, tiled=True)
    for hop in range(reach - 1, 0, -1):
        left = along_ring(add_on(dense[ring - hop], left), -1)
        if hop > 1:
            right = along_ring(add_on(dense[hop - 1], right), 1)
    own, other = call(
        close_kernel,
        "close",
        (shape((width, rows), F32), shape((width, rows), BF)),
        [SMEM] + [VMEM] * 4,
        (VMEM, VMEM),
        flops=CLOSE_COST,
    )(half.reshape(1), grad_pre, dense[0], right, left)
    other = across(other)
    from_cuts = call(
        gather_kernel, "gather", shape((width, rows), F32), [SMEM, SMEM, VMEM], VMEM, moved=2 << 20
    )(send_to, is_live, returned)
    grad_features = call(
        last_kernel, "last", shape((rows, width), BF), [VMEM] * 4, VMEM
    )(own, other, from_cuts, weight)
    return (hidden, grad_features)


def solution(mesh):
    in_specs = (
        P(("dom", "blk"), None),
        P(),
        P(),
        P(("dom", "blk"), None),
        P("dom", "blk", None, None, None, None),
        P("dom", "blk", None, None),
        P("dom", "blk", None),
        P("dom", "blk", None, None, None),
        P("dom", "blk", None),
        P("dom", "blk", None),
        P("dom", "blk", None),
    )
    out_specs = (P(("dom", "blk"), None), P(("dom", "blk"), None))
    return jax.shard_map(
        on_device, mesh=mesh, in_specs=in_specs, out_specs=out_specs, check_vma=False
    )
```

```python
import jax
import jax.numpy as jnp
from jax import lax
from jax.experimental import pallas as pl
from jax.experimental.pallas import tpu as pltpu
from jax.sharding import PartitionSpec as P

BF, F32 = jnp.bfloat16, jnp.float32
TILE = 128
FAR = 2
CHUNKS = 8
VMEM_LIMIT = 16 * 1024 * 1024
PAIR_COST = 100_000_000_000
CLOSE_COST = 26_500_000_000
CUT_COST = 2_000_000_000


def spec(space):
    return pl.BlockSpec(memory_space=space)


SMEM, VMEM, HBM = spec(pltpu.SMEM), spec(pltpu.VMEM), spec(pltpu.HBM)


def call(kernel, name, out_shape, in_specs, out_specs, scratch=(), flops=0, moved=0):
    return pl.pallas_call(
        kernel,
        out_shape=out_shape,
        in_specs=in_specs,
        out_specs=out_specs,
        scratch_shapes=scratch,
        compiler_params=pltpu.CompilerParams(vmem_limit_bytes=VMEM_LIMIT),
        cost_estimate=pl.CostEstimate(flops=flops, bytes_accessed=moved, transcendentals=0),
        name=name,
    )


def in_hbm(value):
    return pltpu.with_memory_space_constraint(value, pltpu.HBM)


def product(left, right):
    return jnp.dot(left, right, preferred_element_type=F32)


def silu_parts(preact):
    sigmoid = 1.0 / (1.0 + jnp.exp(-preact))
    return (preact * sigmoid, sigmoid * (1.0 + preact * (1.0 - sigmoid)))


def project_kernel(features_hbm, weight_hbm, projected_ref, features, weight, sems):
    copies = [
        pltpu.make_async_copy(features_hbm, features, sems.at[0]),
        pltpu.make_async_copy(weight_hbm, weight, sems.at[1]),
    ]
    for copy in copies:
        copy.start()
    for copy in copies:
        copy.wait()
    projected_ref[...] = product(features[...], weight[...]).astype(BF)


def fill_kernel(
    blk_hbm, live_hbm, projected_ref, outgoing_hbm, blk_ref, live_ref, zeros, load_sems, sems
):
    parts = outgoing_hbm.shape[0]
    loads = [
        pltpu.make_async_copy(blk_hbm, blk_ref, load_sems.at[0]),
        pltpu.make_async_copy(live_hbm, live_ref, load_sems.at[1]),
    ]
    for copy in loads:
        copy.start()
    zeros[...] = jnp.zeros(zeros.shape, BF)
    for copy in loads:
        copy.wait()

    def start(part, carried):
        @pl.when(live_ref[part] > 0)
        def _():
            row = pl.multiple_of(blk_ref[part] * TILE, TILE)
            pltpu.make_async_copy(
                projected_ref.at[pl.ds(row, TILE)], outgoing_hbm.at[part], sems.at[part]
            ).start()

        @pl.when(live_ref[part] <= 0)
        def _():
            pltpu.make_async_copy(zeros, outgoing_hbm.at[part], sems.at[part]).start()

        return carried

    def wait(part, carried):
        pltpu.make_async_copy(zeros, outgoing_hbm.at[part], sems.at[part]).wait()
        return carried

    lax.fori_loop(0, parts, start, 0)
    lax.fori_loop(0, parts, wait, 0)


def spread_kernel(ring, blocks, pos_ref, count_ref, place_ref, tiles_ref, *outs):
    rows = blocks * TILE
    place = place_ref[0]
    for offset in range(ring):
        dense = outs[offset]
        dense[...] = jnp.zeros(dense.shape, BF)
        spot = lax.rem(place + offset, ring)
        for half in range(FAR):
            source = half * ring + spot

            def put(slot, carried, dense=dense, half=half, source=source):
                position = pos_ref[source * tiles_ref.shape[1] + slot]
                target = pl.multiple_of(position // blocks * TILE, TILE)
                origin = pl.multiple_of(half * rows + position % blocks * TILE, TILE)
                dense[pl.ds(target, TILE), pl.ds(origin, TILE)] = tiles_ref[source, slot]
                return carried

            lax.fori_loop(0, count_ref[source], put, 0)


def spread_cut_kernel(dst_ref, cut_ref, dense_hbm, dense, sem):
    chunks, _, columns = dense.shape
    chunk = columns // TILE
    dense[...] = jnp.zeros(dense.shape, BF)

    def put(part, carried):
        target = pl.multiple_of(dst_ref[part] * TILE, TILE)
        origin = pl.multiple_of(lax.rem(part, chunk) * TILE, TILE)
        dense[lax.div(part, chunk), pl.ds(target, TILE), pl.ds(origin, TILE)] = cut_ref[part]
        return carried

    lax.fori_loop(0, chunks * chunk, put, 0)
    copy = pltpu.make_async_copy(dense, dense_hbm, sem)
    copy.start()
    copy.wait()


def pair_kernel(half_ref, own_ref, other_ref, pair_ref):
    rows = own_ref.shape[0]
    place = pl.multiple_of(half_ref[0] * rows, TILE)
    pair_ref[pl.ds(place, rows)] = own_ref[...]
    pair_ref[pl.ds(pl.multiple_of(rows - place, TILE), rows)] = other_ref[...]


def cut_sum_kernel(cut_hbm, far_hbm, total_ref, cut, far, sems):
    chunks = cut.shape[0]
    chunk = far.shape[0] // chunks
    width = far.shape[2]
    copies = []
    for piece in range(chunks):
        span = pl.ds(piece * chunk, chunk)
        copies.append(
            (
                pltpu.make_async_copy(cut_hbm.at[piece], cut.at[piece], sems.at[piece]),
                pltpu.make_async_copy(far_hbm.at[span], far.at[span], sems.at[chunks + piece]),
            )
        )
    for pair in copies:
        for copy in pair:
            copy.start()
    for piece in range(chunks):
        for copy in copies[piece]:
            copy.wait()
        arrived = far[pl.ds(piece * chunk, chunk)].reshape(chunk * TILE, width)
        term = product(cut[piece], arrived)
        total_ref[...] = term if piece == 0 else total_ref[...] + term


def middle_kernel(
    sum_ref,
    cut_sum_ref,
    last_ref,
    bias_ref,
    cotangent_ref,
    far_mat_ref,
    near_mat_ref,
    cut_hbm,
    hidden_ref,
    grad_ref,
    left_hbm,
    right_hbm,
    terms_hbm,
    messages,
    cut,
    terms,
    sems,
):
    chunks = cut.shape[0]
    chunk = terms.shape[0] // chunks
    loads = [
        pltpu.make_async_copy(cut_hbm.at[piece], cut.at[piece], sems.at[piece])
        for piece in range(chunks)
    ]
    for copy in loads:
        copy.start()
    total = sum_ref[...] + cut_sum_ref[...] + product(far_mat_ref[...], last_ref[...])
    activated, derivative = silu_parts(total + bias_ref[...])
    hidden_ref[...] = activated.astype(BF)
    grad = (cotangent_ref[...].astype(F32) * derivative).T.astype(BF)
    grad_ref[...] = grad
    stores = []
    for place, (mat_ref, out_hbm) in enumerate(
        ((far_mat_ref, left_hbm), (near_mat_ref, right_hbm))
    ):
        messages[place] = product(grad, mat_ref[...]).astype(BF)
        stores.append(
            pltpu.make_async_copy(messages.at[place], out_hbm, sems.at[2 * chunks + place])
        )
        stores[-1].start()
    for piece in range(chunks):
        loads[piece].wait()
        result = product(grad, cut[piece]).astype(BF)
        for slot in range(chunk):
            terms[piece * chunk + slot] = result[:, slot * TILE : (slot + 1) * TILE]
        span = pl.ds(piece * chunk, chunk)
        stores.append(
            pltpu.make_async_copy(terms.at[span], terms_hbm.at[span], sems.at[chunks + piece])
        )
        stores[-1].start()
    for copy in stores:
        copy.wait()


def gather_kernel(blk_ref, live_ref, arrived_ref, total_ref):
    total_ref[...] = jnp.zeros(total_ref.shape, F32)

    def add(part, carried):
        @pl.when(live_ref[part] > 0)
        def _():
            columns = pl.ds(pl.multiple_of(blk_ref[part] * TILE, TILE), TILE)
            total_ref[:, columns] += arrived_ref[part].astype(F32)

        return carried

    lax.fori_loop(0, arrived_ref.shape[0], add, 0)


def hop_kernel(grad_ref, mat_ref, arrived_ref, out_ref):
    term = product(grad_ref[...], mat_ref[...]) + arrived_ref[...].astype(F32)
    out_ref[...] = term.astype(BF)


def close_kernel(half_ref, grad_ref, mat_ref, left_ref, right_ref, own_ref, other_ref):
    rows = grad_ref.shape[1]
    mine = pl.ds(pl.multiple_of(half_ref[0] * rows, TILE), rows)
    theirs = pl.ds(pl.multiple_of((1 - half_ref[0]) * rows, TILE), rows)

    def total(columns):
        arrived = left_ref[:, columns].astype(F32) + right_ref[:, columns].astype(F32)
        return product(grad_ref[...], mat_ref[:, columns]) + arrived

    other_ref[...] = total(theirs).astype(BF)
    own_ref[...] = total(mine)


def last_kernel(own_ref, other_ref, cut_ref, weight_ref, out_ref):
    total = own_ref[...] + other_ref[...].astype(F32) + cut_ref[...]
    out_ref[...] = lax.dot_general(
        total.T.astype(BF), weight_ref[...], (((1,), (1,)), ((), ())), preferred_element_type=F32
    ).astype(BF)


def on_device(
    features,
    weight,
    bias,
    cotangent,
    in_tiles,
    in_pos,
    in_count,
    cut_tiles,
    send_blk,
    send_live,
    recv_dst,
):
    rows, width = features.shape
    blocks = rows // TILE
    peers = lax.axis_size("blk")
    parts = lax.axis_size("dom")
    ring = peers // FAR
    reach = ring // 2
    me = lax.axis_index("blk")
    place, half = me % ring, me // ring
    wide = FAR * rows
    chunks = min(CHUNKS, parts)
    send_to, is_live, dst = send_blk[0, 0], send_live[0, 0], recv_dst[0, 0]
    shape = jax.ShapeDtypeStruct

    def along_ring(value, by):
        moves = [
            (side * ring + spot, side * ring + (spot + by) % ring)
            for side in range(FAR)
            for spot in range(ring)
        ]
        return lax.ppermute(value, "blk", moves)

    def across(value):
        return lax.ppermute(value, "blk", [(i, (i + ring) % peers) for i in range(peers)])

    projected = call(
        project_kernel,
        "project",
        shape((rows, width), BF),
        [HBM, HBM],
        VMEM,
        [
            pltpu.VMEM(features.shape, BF),
            pltpu.VMEM(weight.shape, BF),
            pltpu.SemaphoreType.DMA((2,)),
        ],
    )(in_hbm(features), in_hbm(weight))
    partner = across(projected)
    outgoing = call(
        fill_kernel,
        "fill",
        pltpu.HBM((parts, TILE, width), BF),
        [HBM, HBM, VMEM],
        HBM,
        [
            pltpu.SMEM((parts,), jnp.int32),
            pltpu.SMEM((parts,), jnp.int32),
            pltpu.VMEM((TILE, width), BF),
            pltpu.SemaphoreType.DMA((2,)),
            pltpu.SemaphoreType.DMA((parts,)),
        ],
    )(in_hbm(send_to), in_hbm(is_live), projected)
    incoming = lax.all_to_all(outgoing, "dom", split_axis=0, concat_axis=0, tiled=True)

    dense = call(
        lambda *refs: spread_kernel(ring, blocks, *refs),
        "spread",
        tuple([shape((rows, wide), BF)] * ring),
        [SMEM, SMEM, SMEM, VMEM],
        tuple([VMEM] * ring),
        moved=10 << 20,
    )(in_pos[0, 0].reshape(-1), in_count[0, 0], place.reshape(1), in_tiles[0, 0])
    dense_cut = call(
        spread_cut_kernel,
        "spread_cut",
        pltpu.HBM((chunks, rows, parts // chunks * TILE), BF),
        [SMEM, VMEM],
        HBM,
        [
            pltpu.VMEM((chunks, rows, parts // chunks * TILE), BF),
            pltpu.SemaphoreType.DMA,
        ],
        moved=6 << 20,
    )(dst, cut_tiles[0, 0])

    pair = call(
        pair_kernel, "pair", shape((wide, width), BF), [SMEM, VMEM, VMEM], VMEM, flops=PAIR_COST
    )(half.reshape(1), projected, partner)
    running = product(dense[0], pair)
    right = left = pair
    for hop in range(1, reach):
        right, left = along_ring(right, 1), along_ring(left, -1)
        running = running + product(dense[ring - hop], right)
        running = running + product(dense[hop], left)
    left = along_ring(left, -1)
    cut_sum = call(
        cut_sum_kernel,
        "cut_sum",
        shape((rows, width), F32),
        [HBM, HBM],
        VMEM,
        [
            pltpu.VMEM(dense_cut.shape, BF),
            pltpu.VMEM((parts, TILE, width), BF),
            pltpu.SemaphoreType.DMA((2 * chunks,)),
        ],
        flops=CUT_COST,
    )(in_hbm(dense_cut), in_hbm(incoming))

    hidden, grad_pre, left, right, terms = call(
        middle_kernel,
        "middle",
        (shape((rows, width), BF), shape((width, rows), BF))
        + (pltpu.HBM((width, wide), BF),) * 2
        + (pltpu.HBM((parts, width, TILE), BF),),
        [VMEM] * 7 + [HBM],
        (VMEM,) * 2 + (HBM,) * 3,
        [
            pltpu.VMEM((2, width, wide), BF),
            pltpu.VMEM(dense_cut.shape, BF),
            pltpu.VMEM((parts, width, TILE), BF),
            pltpu.SemaphoreType.DMA((2 * chunks + 2,)),
        ],
    )(
        running,
        cut_sum,
        left,
        bias.reshape(1, width),
        cotangent,
        dense[reach],
        dense[reach - 1],
        in_hbm(dense_cut),
    )

    def add_on(mat, arrived):
        return call(hop_kernel, "hop", shape((width, wide), BF), [VMEM] * 3, VMEM)(
            grad_pre, mat, arrived
        )

    left, right = along_ring(left, -1), along_ring(right, 1)
    returned = lax.all_to_all(terms, "dom", split_axis=0, concat_axis=0, tiled=True)
    for hop in range(reach - 1, 0, -1):
        left = along_ring(add_on(dense[ring - hop], left), -1)
        if hop > 1:
            right = along_ring(add_on(dense[hop - 1], right), 1)
    own, other = call(
        close_kernel,
        "close",
        (shape((width, rows), F32), shape((width, rows), BF)),
        [SMEM] + [VMEM] * 4,
        (VMEM, VMEM),
        flops=CLOSE_COST,
    )(half.reshape(1), grad_pre, dense[0], right, left)
    other = across(other)
    from_cuts = call(
        gather_kernel, "gather", shape((width, rows), F32), [SMEM, SMEM, VMEM], VMEM, moved=2 << 20
    )(send_to, is_live, returned)
    grad_features = call(
        last_kernel, "last", shape((rows, width), BF), [VMEM] * 4, VMEM
    )(own, other, from_cuts, weight)
    return (hidden, grad_features)


def solution(mesh):
    in_specs = (
        P(("dom", "blk"), None),
        P(),
        P(),
        P(("dom", "blk"), None),
        P("dom", "blk", None, None, None, None),
        P("dom", "blk", None, None),
        P("dom", "blk", None),
        P("dom", "blk", None, None, None),
        P("dom", "blk", None),
        P("dom", "blk", None),
        P("dom", "blk", None),
    )
    out_specs = (P(("dom", "blk"), None), P(("dom", "blk"), None))
    return jax.shard_map(
        on_device, mesh=mesh, in_specs=in_specs, out_specs=out_specs, check_vma=False
    )
```

```python
import jax
import jax.numpy as jnp
from jax import lax
from jax.experimental import pallas as pl
from jax.experimental.pallas import tpu as pltpu
from jax.sharding import PartitionSpec as P

BF, F32 = jnp.bfloat16, jnp.float32
TILE = 128
FAR = 2
CHUNKS = 8
VMEM_LIMIT = 16 * 1024 * 1024
PAIR_COST = 100_000_000_000
CLOSE_COST = 26_500_000_000
CUT_COST = 2_000_000_000


def spec(space):
    return pl.BlockSpec(memory_space=space)


SMEM, VMEM, HBM = spec(pltpu.SMEM), spec(pltpu.VMEM), spec(pltpu.HBM)


def call(kernel, name, out_shape, in_specs, out_specs, scratch=(), flops=0, moved=0):
    return pl.pallas_call(
        kernel,
        out_shape=out_shape,
        in_specs=in_specs,
        out_specs=out_specs,
        scratch_shapes=scratch,
        compiler_params=pltpu.CompilerParams(vmem_limit_bytes=VMEM_LIMIT),
        cost_estimate=pl.CostEstimate(flops=flops, bytes_accessed=moved, transcendentals=0),
        name=name,
    )


def in_hbm(value):
    return pltpu.with_memory_space_constraint(value, pltpu.HBM)


def product(left, right):
    return jnp.dot(left, right, preferred_element_type=F32)


def silu_parts(preact):
    sigmoid = 1.0 / (1.0 + jnp.exp(-preact))
    return (preact * sigmoid, sigmoid * (1.0 + preact * (1.0 - sigmoid)))


def project_kernel(features_hbm, weight_hbm, projected_ref, features, weight, sems):
    copies = [
        pltpu.make_async_copy(features_hbm, features, sems.at[0]),
        pltpu.make_async_copy(weight_hbm, weight, sems.at[1]),
    ]
    for copy in copies:
        copy.start()
    for copy in copies:
        copy.wait()
    projected_ref[...] = product(features[...], weight[...]).astype(BF)


def fill_kernel(
    blk_hbm, live_hbm, projected_ref, outgoing_hbm, blk_ref, live_ref, zeros, load_sems, sems
):
    parts = outgoing_hbm.shape[0]
    loads = [
        pltpu.make_async_copy(blk_hbm, blk_ref, load_sems.at[0]),
        pltpu.make_async_copy(live_hbm, live_ref, load_sems.at[1]),
    ]
    for copy in loads:
        copy.start()
    zeros[...] = jnp.zeros(zeros.shape, BF)
    for copy in loads:
        copy.wait()

    def start(part, carried):
        @pl.when(live_ref[part] > 0)
        def _():
            row = pl.multiple_of(blk_ref[part] * TILE, TILE)
            pltpu.make_async_copy(
                projected_ref.at[pl.ds(row, TILE)], outgoing_hbm.at[part], sems.at[part]
            ).start()

        @pl.when(live_ref[part] <= 0)
        def _():
            pltpu.make_async_copy(zeros, outgoing_hbm.at[part], sems.at[part]).start()

        return carried

    def wait(part, carried):
        pltpu.make_async_copy(zeros, outgoing_hbm.at[part], sems.at[part]).wait()
        return carried

    lax.fori_loop(0, parts, start, 0)
    lax.fori_loop(0, parts, wait, 0)


def spread_kernel(ring, blocks, pos_ref, count_ref, place_ref, tiles_ref, *outs):
    rows = blocks * TILE
    place, mirrored = place_ref[0], place_ref[1]
    for offset in range(ring):
        dense = outs[offset]
        dense[...] = jnp.zeros(dense.shape, BF)
        spot = lax.rem(place + jnp.where(mirrored > 0, ring - offset, offset), ring)
        for half in range(FAR):
            source = half * ring + spot

            def put(slot, carried, dense=dense, half=half, source=source):
                position = pos_ref[source * tiles_ref.shape[1] + slot]
                target = pl.multiple_of(position // blocks * TILE, TILE)
                origin = pl.multiple_of(half * rows + position % blocks * TILE, TILE)
                dense[pl.ds(target, TILE), pl.ds(origin, TILE)] = tiles_ref[source, slot]
                return carried

            lax.fori_loop(0, count_ref[source], put, 0)


def spread_cut_kernel(dst_ref, cut_ref, dense_hbm, dense, sem):
    chunks, _, columns = dense.shape
    chunk = columns // TILE
    dense[...] = jnp.zeros(dense.shape, BF)

    def put(part, carried):
        target = pl.multiple_of(dst_ref[part] * TILE, TILE)
        origin = pl.multiple_of(lax.rem(part, chunk) * TILE, TILE)
        dense[lax.div(part, chunk), pl.ds(target, TILE), pl.ds(origin, TILE)] = cut_ref[part]
        return carried

    lax.fori_loop(0, chunks * chunk, put, 0)
    copy = pltpu.make_async_copy(dense, dense_hbm, sem)
    copy.start()
    copy.wait()


def pair_kernel(half_ref, own_ref, other_ref, pair_ref):
    rows = own_ref.shape[0]
    place = pl.multiple_of(half_ref[0] * rows, TILE)
    pair_ref[pl.ds(place, rows)] = own_ref[...]
    pair_ref[pl.ds(pl.multiple_of(rows - place, TILE), rows)] = other_ref[...]


def cut_sum_kernel(cut_hbm, far_hbm, total_ref, cut, far, sems):
    chunks = cut.shape[0]
    chunk = far.shape[0] // chunks
    width = far.shape[2]
    copies = []
    for piece in range(chunks):
        span = pl.ds(piece * chunk, chunk)
        copies.append(
            (
                pltpu.make_async_copy(cut_hbm.at[piece], cut.at[piece], sems.at[piece]),
                pltpu.make_async_copy(far_hbm.at[span], far.at[span], sems.at[chunks + piece]),
            )
        )
    for pair in copies:
        for copy in pair:
            copy.start()
    for piece in range(chunks):
        for copy in copies[piece]:
            copy.wait()
        arrived = far[pl.ds(piece * chunk, chunk)].reshape(chunk * TILE, width)
        term = product(cut[piece], arrived)
        total_ref[...] = term if piece == 0 else total_ref[...] + term


def middle_kernel(
    sum_ref,
    cut_sum_ref,
    last_ref,
    bias_ref,
    cotangent_ref,
    far_mat_ref,
    near_mat_ref,
    cut_hbm,
    hidden_hbm,
    grad_hbm,
    left_hbm,
    right_hbm,
    terms_hbm,
    hidden,
    gradient,
    messages,
    cut,
    terms,
    sems,
):
    chunks = cut.shape[0]
    chunk = terms.shape[0] // chunks
    loads = [
        pltpu.make_async_copy(cut_hbm.at[piece], cut.at[piece], sems.at[piece])
        for piece in range(chunks)
    ]
    for copy in loads:
        copy.start()
    total = sum_ref[...] + cut_sum_ref[...] + product(far_mat_ref[...], last_ref[...])
    activated, derivative = silu_parts(total + bias_ref[...])
    hidden[...] = activated.astype(BF)
    grad = (cotangent_ref[...].astype(F32) * derivative).T.astype(BF)
    gradient[...] = grad
    stores = [
        pltpu.make_async_copy(hidden, hidden_hbm, sems.at[2 * chunks + 2]),
        pltpu.make_async_copy(gradient, grad_hbm, sems.at[2 * chunks + 3]),
    ]
    for copy in stores:
        copy.start()
    for place, (mat_ref, out_hbm) in enumerate(
        ((far_mat_ref, left_hbm), (near_mat_ref, right_hbm))
    ):
        messages[place] = product(grad, mat_ref[...]).astype(BF)
        stores.append(
            pltpu.make_async_copy(messages.at[place], out_hbm, sems.at[2 * chunks + place])
        )
        stores[-1].start()
    for piece in range(chunks):
        loads[piece].wait()
        result = product(grad, cut[piece]).astype(BF)
        for slot in range(chunk):
            terms[piece * chunk + slot] = result[:, slot * TILE : (slot + 1) * TILE]
        span = pl.ds(piece * chunk, chunk)
        stores.append(
            pltpu.make_async_copy(terms.at[span], terms_hbm.at[span], sems.at[chunks + piece])
        )
        stores[-1].start()
    for copy in stores:
        copy.wait()


def gather_kernel(blk_ref, live_ref, arrived_ref, total_ref):
    total_ref[...] = jnp.zeros(total_ref.shape, F32)

    def add(part, carried):
        @pl.when(live_ref[part] > 0)
        def _():
            columns = pl.ds(pl.multiple_of(blk_ref[part] * TILE, TILE), TILE)
            total_ref[:, columns] += arrived_ref[part].astype(F32)

        return carried

    lax.fori_loop(0, arrived_ref.shape[0], add, 0)


def hop_kernel(grad_ref, mat_ref, arrived_ref, out_ref):
    term = product(grad_ref[...], mat_ref[...]) + arrived_ref[...].astype(F32)
    out_ref[...] = term.astype(BF)


def close_kernel(half_ref, grad_ref, mat_ref, left_ref, right_ref, own_ref, other_ref):
    rows = grad_ref.shape[1]
    mine = pl.ds(pl.multiple_of(half_ref[0] * rows, TILE), rows)
    theirs = pl.ds(pl.multiple_of((1 - half_ref[0]) * rows, TILE), rows)

    def total(columns):
        arrived = left_ref[:, columns].astype(F32) + right_ref[:, columns].astype(F32)
        return product(grad_ref[...], mat_ref[:, columns]) + arrived

    other_ref[...] = total(theirs).astype(BF)
    own_ref[...] = total(mine)


def last_kernel(own_ref, other_ref, cut_ref, weight_ref, out_ref):
    total = own_ref[...] + other_ref[...].astype(F32) + cut_ref[...]
    out_ref[...] = lax.dot_general(
        total.T.astype(BF), weight_ref[...], (((1,), (1,)), ((), ())), preferred_element_type=F32
    ).astype(BF)


def on_device(
    features,
    weight,
    bias,
    cotangent,
    in_tiles,
    in_pos,
    in_count,
    cut_tiles,
    send_blk,
    send_live,
    recv_dst,
):
    rows, width = features.shape
    blocks = rows // TILE
    peers = lax.axis_size("blk")
    parts = lax.axis_size("dom")
    ring = peers // FAR
    reach = ring // 2
    me = lax.axis_index("blk")
    place, half = me % ring, me // ring
    wide = FAR * rows
    chunks = min(CHUNKS, parts)
    send_to, is_live, dst = send_blk[0, 0], send_live[0, 0], recv_dst[0, 0]
    shape = jax.ShapeDtypeStruct

    mirrored = lax.axis_index("dom") % 2

    def along_ring(value, by):
        moves = [
            (first + spot, first + (spot + (by if part % 2 == 0 else -by)) % ring)
            for part in range(parts)
            for first in range(part * peers, (part + 1) * peers, ring)
            for spot in range(ring)
        ]
        return lax.ppermute(value, ("dom", "blk"), moves)

    def across(value):
        return lax.ppermute(value, "blk", [(i, (i + ring) % peers) for i in range(peers)])

    projected = call(
        project_kernel,
        "project",
        shape((rows, width), BF),
        [HBM, HBM],
        VMEM,
        [
            pltpu.VMEM(features.shape, BF),
            pltpu.VMEM(weight.shape, BF),
            pltpu.SemaphoreType.DMA((2,)),
        ],
    )(in_hbm(features), in_hbm(weight))
    partner = across(projected)
    outgoing = call(
        fill_kernel,
        "fill",
        pltpu.HBM((parts, TILE, width), BF),
        [HBM, HBM, VMEM],
        HBM,
        [
            pltpu.SMEM((parts,), jnp.int32),
            pltpu.SMEM((parts,), jnp.int32),
            pltpu.VMEM((TILE, width), BF),
            pltpu.SemaphoreType.DMA((2,)),
            pltpu.SemaphoreType.DMA((parts,)),
        ],
    )(in_hbm(send_to), in_hbm(is_live), projected)
    incoming = lax.all_to_all(outgoing, "dom", split_axis=0, concat_axis=0, tiled=True)

    dense = call(
        lambda *refs: spread_kernel(ring, blocks, *refs),
        "spread",
        tuple([shape((rows, wide), BF)] * ring),
        [SMEM, SMEM, SMEM, VMEM],
        tuple([VMEM] * ring),
        moved=10 << 20,
    )(in_pos[0, 0].reshape(-1), in_count[0, 0], jnp.stack([place, mirrored]), in_tiles[0, 0])
    dense_cut = call(
        spread_cut_kernel,
        "spread_cut",
        pltpu.HBM((chunks, rows, parts // chunks * TILE), BF),
        [SMEM, VMEM],
        HBM,
        [
            pltpu.VMEM((chunks, rows, parts // chunks * TILE), BF),
            pltpu.SemaphoreType.DMA,
        ],
        moved=6 << 20,
    )(dst, cut_tiles[0, 0])

    pair = call(
        pair_kernel, "pair", shape((wide, width), BF), [SMEM, VMEM, VMEM], VMEM, flops=PAIR_COST
    )(half.reshape(1), projected, partner)
    running = product(dense[0], pair)
    right = left = pair
    for hop in range(1, reach):
        right, left = along_ring(right, 1), along_ring(left, -1)
        running = running + product(dense[ring - hop], right)
        running = running + product(dense[hop], left)
    left = along_ring(left, -1)
    cut_sum = call(
        cut_sum_kernel,
        "cut_sum",
        shape((rows, width), F32),
        [HBM, HBM],
        VMEM,
        [
            pltpu.VMEM(dense_cut.shape, BF),
            pltpu.VMEM((parts, TILE, width), BF),
            pltpu.SemaphoreType.DMA((2 * chunks,)),
        ],
        flops=CUT_COST,
    )(in_hbm(dense_cut), in_hbm(incoming))

    hidden, grad_pre, left, right, terms = call(
        middle_kernel,
        "middle",
        (pltpu.HBM((rows, width), BF), pltpu.HBM((width, rows), BF))
        + (pltpu.HBM((width, wide), BF),) * 2
        + (pltpu.HBM((parts, width, TILE), BF),),
        [VMEM] * 7 + [HBM],
        (HBM,) * 5,
        [
            pltpu.VMEM((rows, width), BF),
            pltpu.VMEM((width, rows), BF),
            pltpu.VMEM((2, width, wide), BF),
            pltpu.VMEM(dense_cut.shape, BF),
            pltpu.VMEM((parts, width, TILE), BF),
            pltpu.SemaphoreType.DMA((2 * chunks + 4,)),
        ],
    )(
        running,
        cut_sum,
        left,
        bias.reshape(1, width),
        cotangent,
        dense[reach],
        dense[reach - 1],
        in_hbm(dense_cut),
    )

    def add_on(mat, arrived):
        return call(hop_kernel, "hop", shape((width, wide), BF), [VMEM] * 3, VMEM)(
            grad_pre, mat, arrived
        )

    left, right = along_ring(left, -1), along_ring(right, 1)
    returned = lax.all_to_all(terms, "dom", split_axis=0, concat_axis=0, tiled=True)
    for hop in range(reach - 1, 0, -1):
        left = along_ring(add_on(dense[ring - hop], left), -1)
        if hop > 1:
            right = along_ring(add_on(dense[hop - 1], right), 1)
    own, other = call(
        close_kernel,
        "close",
        (shape((width, rows), F32), shape((width, rows), BF)),
        [SMEM] + [VMEM] * 4,
        (VMEM, VMEM),
        flops=CLOSE_COST,
    )(half.reshape(1), grad_pre, dense[0], right, left)
    other = across(other)
    from_cuts = call(
        gather_kernel, "gather", shape((width, rows), F32), [SMEM, SMEM, VMEM], VMEM, moved=2 << 20
    )(send_to, is_live, returned)
    grad_features = call(
        last_kernel, "last", shape((rows, width), BF), [VMEM] * 4, VMEM
    )(own, other, from_cuts, weight)
    return (hidden, grad_features)


def solution(mesh):
    in_specs = (
        P(("dom", "blk"), None),
        P(),
        P(),
        P(("dom", "blk"), None),
        P("dom", "blk", None, None, None, None),
        P("dom", "blk", None, None),
        P("dom", "blk", None),
        P("dom", "blk", None, None, None),
        P("dom", "blk", None),
        P("dom", "blk", None),
        P("dom", "blk", None),
    )
    out_specs = (P(("dom", "blk"), None), P(("dom", "blk"), None))
    return jax.shard_map(
        on_device, mesh=mesh, in_specs=in_specs, out_specs=out_specs, check_vma=False
    )
```

```python
import jax
import jax.numpy as jnp
from jax import lax
from jax.experimental import pallas as pl
from jax.experimental.pallas import tpu as pltpu
from jax.sharding import PartitionSpec as P

BF, F32 = jnp.bfloat16, jnp.float32
TILE = 128
FAR = 2
CHUNKS = 8
VMEM_LIMIT = 16 * 1024 * 1024
CLOSE_COST = 26_500_000_000
CUT_COST = 2_000_000_000


def spec(space):
    return pl.BlockSpec(memory_space=space)


SMEM, VMEM, HBM = spec(pltpu.SMEM), spec(pltpu.VMEM), spec(pltpu.HBM)


def call(kernel, name, out_shape, in_specs, out_specs, scratch=(), flops=0, moved=0):
    return pl.pallas_call(
        kernel,
        out_shape=out_shape,
        in_specs=in_specs,
        out_specs=out_specs,
        scratch_shapes=scratch,
        compiler_params=pltpu.CompilerParams(vmem_limit_bytes=VMEM_LIMIT),
        cost_estimate=pl.CostEstimate(flops=flops, bytes_accessed=moved, transcendentals=0),
        name=name,
    )


def in_hbm(value):
    return pltpu.with_memory_space_constraint(value, pltpu.HBM)


def product(left, right):
    return jnp.dot(left, right, preferred_element_type=F32)


def silu_parts(preact):
    sigmoid = 1.0 / (1.0 + jnp.exp(-preact))
    return (preact * sigmoid, sigmoid * (1.0 + preact * (1.0 - sigmoid)))


def project_kernel(features_hbm, weight_hbm, projected_ref, features, weight, sems):
    copies = [
        pltpu.make_async_copy(features_hbm, features, sems.at[0]),
        pltpu.make_async_copy(weight_hbm, weight, sems.at[1]),
    ]
    for copy in copies:
        copy.start()
    for copy in copies:
        copy.wait()
    projected_ref[...] = product(features[...], weight[...]).astype(BF)


def fill_kernel(
    blk_hbm, live_hbm, projected_ref, outgoing_hbm, blk_ref, live_ref, zeros, load_sems, sems
):
    parts = outgoing_hbm.shape[0]
    loads = [
        pltpu.make_async_copy(blk_hbm, blk_ref, load_sems.at[0]),
        pltpu.make_async_copy(live_hbm, live_ref, load_sems.at[1]),
    ]
    for copy in loads:
        copy.start()
    zeros[...] = jnp.zeros(zeros.shape, BF)
    for copy in loads:
        copy.wait()

    def start(part, carried):
        @pl.when(live_ref[part] > 0)
        def _():
            row = pl.multiple_of(blk_ref[part] * TILE, TILE)
            pltpu.make_async_copy(
                projected_ref.at[pl.ds(row, TILE)], outgoing_hbm.at[part], sems.at[part]
            ).start()

        @pl.when(live_ref[part] <= 0)
        def _():
            pltpu.make_async_copy(zeros, outgoing_hbm.at[part], sems.at[part]).start()

        return carried

    def wait(part, carried):
        pltpu.make_async_copy(zeros, outgoing_hbm.at[part], sems.at[part]).wait()
        return carried

    lax.fori_loop(0, parts, start, 0)
    lax.fori_loop(0, parts, wait, 0)


def spread_kernel(ring, blocks, pos_ref, count_ref, place_ref, tiles_ref, *outs):
    rows = blocks * TILE
    place, mine = place_ref[0], place_ref[1]
    for offset in range(ring):
        dense = outs[offset]
        dense[...] = jnp.zeros(dense.shape, BF)
        spot = lax.rem(place + offset, ring)
        for half in range(FAR):
            source = (mine if half == 0 else 1 - mine) * ring + spot

            def put(slot, carried, dense=dense, half=half, source=source):
                position = pos_ref[source * tiles_ref.shape[1] + slot]
                target = pl.multiple_of(position // blocks * TILE, TILE)
                origin = pl.multiple_of(half * rows + position % blocks * TILE, TILE)
                dense[pl.ds(target, TILE), pl.ds(origin, TILE)] = tiles_ref[source, slot]
                return carried

            lax.fori_loop(0, count_ref[source], put, 0)


def spread_cut_kernel(dst_ref, cut_ref, dense_hbm, dense, sem):
    chunks, _, columns = dense.shape
    chunk = columns // TILE
    dense[...] = jnp.zeros(dense.shape, BF)

    def put(part, carried):
        target = pl.multiple_of(dst_ref[part] * TILE, TILE)
        origin = pl.multiple_of(lax.rem(part, chunk) * TILE, TILE)
        dense[lax.div(part, chunk), pl.ds(target, TILE), pl.ds(origin, TILE)] = cut_ref[part]
        return carried

    lax.fori_loop(0, chunks * chunk, put, 0)
    copy = pltpu.make_async_copy(dense, dense_hbm, sem)
    copy.start()
    copy.wait()


def cut_sum_kernel(cut_hbm, far_hbm, total_ref, cut, far, sems):
    chunks = cut.shape[0]
    chunk = far.shape[0] // chunks
    width = far.shape[2]
    copies = []
    for piece in range(chunks):
        span = pl.ds(piece * chunk, chunk)
        copies.append(
            (
                pltpu.make_async_copy(cut_hbm.at[piece], cut.at[piece], sems.at[piece]),
                pltpu.make_async_copy(far_hbm.at[span], far.at[span], sems.at[chunks + piece]),
            )
        )
    for pair in copies:
        for copy in pair:
            copy.start()
    for piece in range(chunks):
        for copy in copies[piece]:
            copy.wait()
        arrived = far[pl.ds(piece * chunk, chunk)].reshape(chunk * TILE, width)
        term = product(cut[piece], arrived)
        total_ref[...] = term if piece == 0 else total_ref[...] + term


def middle_kernel(
    sum_ref,
    cut_sum_ref,
    own_hbm,
    other_hbm,
    bias_ref,
    cotangent_ref,
    far_mat_ref,
    near_mat_ref,
    cut_hbm,
    hidden_ref,
    grad_ref,
    left_hbm,
    right_hbm,
    terms_hbm,
    arrived,
    messages,
    cut,
    terms,
    sems,
):
    chunks = cut.shape[0]
    chunk = terms.shape[0] // chunks
    last = [
        pltpu.make_async_copy(source, arrived.at[place], sems.at[2 * chunks + 2 + place])
        for place, source in enumerate((own_hbm, other_hbm))
    ]
    for copy in last:
        copy.start()
    loads = [
        pltpu.make_async_copy(cut_hbm.at[piece], cut.at[piece], sems.at[piece])
        for piece in range(chunks)
    ]
    for copy in loads:
        copy.start()
    rows = sum_ref.shape[0]
    total = sum_ref[...] + cut_sum_ref[...]
    for place, copy in enumerate(last):
        copy.wait()
        columns = pl.ds(place * rows, rows)
        total += product(far_mat_ref[:, columns], arrived[place])
    activated, derivative = silu_parts(total + bias_ref[...])
    hidden_ref[...] = activated.astype(BF)
    grad = (cotangent_ref[...].astype(F32) * derivative).T.astype(BF)
    grad_ref[...] = grad
    stores = []
    for place, (mat_ref, out_hbm) in enumerate(
        ((far_mat_ref, left_hbm), (near_mat_ref, right_hbm))
    ):
        messages[place] = product(grad, mat_ref[...]).astype(BF)
        stores.append(
            pltpu.make_async_copy(messages.at[place], out_hbm, sems.at[2 * chunks + place])
        )
        stores[-1].start()
    for piece in range(chunks):
        loads[piece].wait()
        result = product(grad, cut[piece]).astype(BF)
        for slot in range(chunk):
            terms[piece * chunk + slot] = result[:, slot * TILE : (slot + 1) * TILE]
        span = pl.ds(piece * chunk, chunk)
        stores.append(
            pltpu.make_async_copy(terms.at[span], terms_hbm.at[span], sems.at[chunks + piece])
        )
        stores[-1].start()
    for copy in stores:
        copy.wait()


def gather_kernel(blk_ref, live_ref, arrived_ref, total_ref):
    total_ref[...] = jnp.zeros(total_ref.shape, F32)

    def add(part, carried):
        @pl.when(live_ref[part] > 0)
        def _():
            columns = pl.ds(pl.multiple_of(blk_ref[part] * TILE, TILE), TILE)
            total_ref[:, columns] += arrived_ref[part].astype(F32)

        return carried

    lax.fori_loop(0, arrived_ref.shape[0], add, 0)


def hop_kernel(grad_ref, mat_ref, arrived_ref, out_ref):
    term = product(grad_ref[...], mat_ref[...]) + arrived_ref[...].astype(F32)
    out_ref[...] = term.astype(BF)


def close_kernel(grad_ref, mat_ref, left_ref, right_ref, own_ref, other_ref):
    rows = grad_ref.shape[1]

    def total(columns):
        arrived = left_ref[:, columns].astype(F32) + right_ref[:, columns].astype(F32)
        return product(grad_ref[...], mat_ref[:, columns]) + arrived

    other_ref[...] = total(slice(rows, None)).astype(BF)
    own_ref[...] = total(slice(0, rows))


def last_kernel(own_ref, other_ref, cut_ref, weight_ref, out_ref):
    total = own_ref[...] + other_ref[...].astype(F32) + cut_ref[...]
    out_ref[...] = lax.dot_general(
        total.T.astype(BF), weight_ref[...], (((1,), (1,)), ((), ())), preferred_element_type=F32
    ).astype(BF)


def on_device(
    features,
    weight,
    bias,
    cotangent,
    in_tiles,
    in_pos,
    in_count,
    cut_tiles,
    send_blk,
    send_live,
    recv_dst,
):
    rows, width = features.shape
    blocks = rows // TILE
    peers = lax.axis_size("blk")
    parts = lax.axis_size("dom")
    ring = peers // FAR
    reach = ring // 2
    me = lax.axis_index("blk")
    place, half = me % ring, me // ring
    wide = FAR * rows
    chunks = min(CHUNKS, parts)
    send_to, is_live, dst = send_blk[0, 0], send_live[0, 0], recv_dst[0, 0]
    shape = jax.ShapeDtypeStruct

    def along_ring(value, by):
        moves = [
            (side * ring + spot, side * ring + (spot + by) % ring)
            for side in range(FAR)
            for spot in range(ring)
        ]
        return lax.ppermute(value, "blk", moves)

    def across(value):
        return lax.ppermute(value, "blk", [(i, (i + ring) % peers) for i in range(peers)])

    projected = call(
        project_kernel,
        "project",
        shape((rows, width), BF),
        [HBM, HBM],
        VMEM,
        [
            pltpu.VMEM(features.shape, BF),
            pltpu.VMEM(weight.shape, BF),
            pltpu.SemaphoreType.DMA((2,)),
        ],
    )(in_hbm(features), in_hbm(weight))
    partner = across(projected)
    outgoing = call(
        fill_kernel,
        "fill",
        pltpu.HBM((parts, TILE, width), BF),
        [HBM, HBM, VMEM],
        HBM,
        [
            pltpu.SMEM((parts,), jnp.int32),
            pltpu.SMEM((parts,), jnp.int32),
            pltpu.VMEM((TILE, width), BF),
            pltpu.SemaphoreType.DMA((2,)),
            pltpu.SemaphoreType.DMA((parts,)),
        ],
    )(in_hbm(send_to), in_hbm(is_live), projected)
    incoming = lax.all_to_all(outgoing, "dom", split_axis=0, concat_axis=0, tiled=True)

    dense = call(
        lambda *refs: spread_kernel(ring, blocks, *refs),
        "spread",
        tuple([shape((rows, wide), BF)] * ring),
        [SMEM, SMEM, SMEM, VMEM],
        tuple([VMEM] * ring),
        moved=10 << 20,
    )(in_pos[0, 0].reshape(-1), in_count[0, 0], jnp.stack([place, half]), in_tiles[0, 0])
    dense_cut = call(
        spread_cut_kernel,
        "spread_cut",
        pltpu.HBM((chunks, rows, parts // chunks * TILE), BF),
        [SMEM, VMEM],
        HBM,
        [
            pltpu.VMEM((chunks, rows, parts // chunks * TILE), BF),
            pltpu.SemaphoreType.DMA,
        ],
        moved=6 << 20,
    )(dst, cut_tiles[0, 0])

    running = jnp.zeros((rows, width), F32)
    last = []
    for source, columns in ((projected, slice(0, rows)), (partner, slice(rows, wide))):
        running = running + product(dense[0][:, columns], source)
        right = left = source
        for hop in range(1, reach):
            right, left = along_ring(right, 1), along_ring(left, -1)
            running = running + product(dense[ring - hop][:, columns], right)
            running = running + product(dense[hop][:, columns], left)
        last.append(in_hbm(along_ring(left, -1)))
    cut_sum = call(
        cut_sum_kernel,
        "cut_sum",
        shape((rows, width), F32),
        [HBM, HBM],
        VMEM,
        [
            pltpu.VMEM(dense_cut.shape, BF),
            pltpu.VMEM((parts, TILE, width), BF),
            pltpu.SemaphoreType.DMA((2 * chunks,)),
        ],
        flops=CUT_COST,
    )(in_hbm(dense_cut), in_hbm(incoming))

    hidden, grad_pre, left, right, terms = call(
        middle_kernel,
        "middle",
        (shape((rows, width), BF), shape((width, rows), BF))
        + (pltpu.HBM((width, wide), BF),) * 2
        + (pltpu.HBM((parts, width, TILE), BF),),
        [VMEM] * 2 + [HBM] * 2 + [VMEM] * 4 + [HBM],
        (VMEM,) * 2 + (HBM,) * 3,
        [
            pltpu.VMEM((2, rows, width), BF),
            pltpu.VMEM((2, width, wide), BF),
            pltpu.VMEM(dense_cut.shape, BF),
            pltpu.VMEM((parts, width, TILE), BF),
            pltpu.SemaphoreType.DMA((2 * chunks + 4,)),
        ],
    )(
        running,
        cut_sum,
        *last,
        bias.reshape(1, width),
        cotangent,
        dense[reach],
        dense[reach - 1],
        in_hbm(dense_cut),
    )

    def add_on(mat, arrived):
        return call(hop_kernel, "hop", shape((width, wide), BF), [VMEM] * 3, VMEM)(
            grad_pre, mat, arrived
        )

    left, right = along_ring(left, -1), along_ring(right, 1)
    returned = lax.all_to_all(terms, "dom", split_axis=0, concat_axis=0, tiled=True)
    for hop in range(reach - 1, 0, -1):
        left = along_ring(add_on(dense[ring - hop], left), -1)
        if hop > 1:
            right = along_ring(add_on(dense[hop - 1], right), 1)
    own, other = call(
        close_kernel,
        "close",
        (shape((width, rows), F32), shape((width, rows), BF)),
        [VMEM] * 4,
        (VMEM, VMEM),
        flops=CLOSE_COST,
    )(grad_pre, dense[0], right, left)
    other = across(other)
    from_cuts = call(
        gather_kernel, "gather", shape((width, rows), F32), [SMEM, SMEM, VMEM], VMEM, moved=2 << 20
    )(send_to, is_live, returned)
    grad_features = call(
        last_kernel, "last", shape((rows, width), BF), [VMEM] * 4, VMEM
    )(own, other, from_cuts, weight)
    return (hidden, grad_features)


def solution(mesh):
    in_specs = (
        P(("dom", "blk"), None),
        P(),
        P(),
        P(("dom", "blk"), None),
        P("dom", "blk", None, None, None, None),
        P("dom", "blk", None, None),
        P("dom", "blk", None),
        P("dom", "blk", None, None, None),
        P("dom", "blk", None),
        P("dom", "blk", None),
        P("dom", "blk", None),
    )
    out_specs = (P(("dom", "blk"), None), P(("dom", "blk"), None))
    return jax.shard_map(
        on_device, mesh=mesh, in_specs=in_specs, out_specs=out_specs, check_vma=False
    )
```

```python
import jax
import jax.numpy as jnp
from jax import lax
from jax.experimental import pallas as pl
from jax.experimental.pallas import tpu as pltpu
from jax.sharding import PartitionSpec as P

BF, F32 = jnp.bfloat16, jnp.float32
TILE = 128
FAR = 2
CHUNKS = 8
VMEM_LIMIT = 16 * 1024 * 1024
PAIR_COST = 100_000_000_000
CLOSE_COST = 26_500_000_000
CUT_COST = 2_000_000_000


def spec(space):
    return pl.BlockSpec(memory_space=space)


SMEM, VMEM, HBM = spec(pltpu.SMEM), spec(pltpu.VMEM), spec(pltpu.HBM)


def call(kernel, name, out_shape, in_specs, out_specs, scratch=(), flops=0, moved=0):
    return pl.pallas_call(
        kernel,
        out_shape=out_shape,
        in_specs=in_specs,
        out_specs=out_specs,
        scratch_shapes=scratch,
        compiler_params=pltpu.CompilerParams(vmem_limit_bytes=VMEM_LIMIT),
        cost_estimate=pl.CostEstimate(flops=flops, bytes_accessed=moved, transcendentals=0),
        name=name,
    )


def in_hbm(value):
    return pltpu.with_memory_space_constraint(value, pltpu.HBM)


def product(left, right):
    return jnp.dot(left, right, preferred_element_type=F32)


def silu_parts(preact):
    sigmoid = 1.0 / (1.0 + jnp.exp(-preact))
    return (preact * sigmoid, sigmoid * (1.0 + preact * (1.0 - sigmoid)))


def project_kernel(
    blk_hbm,
    live_hbm,
    features_hbm,
    weight_hbm,
    projected_ref,
    outgoing_hbm,
    blk_ref,
    live_ref,
    features,
    weight,
    zeros,
    load_sems,
    sems,
):
    parts = outgoing_hbm.shape[0]
    loads = [
        pltpu.make_async_copy(source, target, load_sems.at[place])
        for place, (source, target) in enumerate(
            (
                (features_hbm, features),
                (weight_hbm, weight),
                (blk_hbm, blk_ref),
                (live_hbm, live_ref),
            )
        )
    ]
    for copy in loads:
        copy.start()
    zeros[...] = jnp.zeros(zeros.shape, BF)
    for copy in loads:
        copy.wait()
    projected_ref[...] = product(features[...], weight[...]).astype(BF)

    def start(part, carried):
        @pl.when(live_ref[part] > 0)
        def _():
            row = pl.multiple_of(blk_ref[part] * TILE, TILE)
            pltpu.make_async_copy(
                projected_ref.at[pl.ds(row, TILE)], outgoing_hbm.at[part], sems.at[part]
            ).start()

        @pl.when(live_ref[part] <= 0)
        def _():
            pltpu.make_async_copy(zeros, outgoing_hbm.at[part], sems.at[part]).start()

        return carried

    def wait(part, carried):
        pltpu.make_async_copy(zeros, outgoing_hbm.at[part], sems.at[part]).wait()
        return carried

    lax.fori_loop(0, parts, start, 0)
    lax.fori_loop(0, parts, wait, 0)


def spread_kernel(ring, blocks, pos_ref, count_ref, place_ref, tiles_ref, *outs):
    rows = blocks * TILE
    place = place_ref[0]
    for offset in range(ring):
        dense = outs[offset]
        dense[...] = jnp.zeros(dense.shape, BF)
        spot = lax.rem(place + offset, ring)
        for half in range(FAR):
            source = half * ring + spot

            def put(slot, carried, dense=dense, half=half, source=source):
                position = pos_ref[source * tiles_ref.shape[1] + slot]
                target = pl.multiple_of(position // blocks * TILE, TILE)
                origin = pl.multiple_of(half * rows + position % blocks * TILE, TILE)
                dense[pl.ds(target, TILE), pl.ds(origin, TILE)] = tiles_ref[source, slot]
                return carried

            lax.fori_loop(0, count_ref[source], put, 0)


def spread_cut_kernel(dst_ref, cut_ref, dense_hbm, dense, sem):
    chunks, _, columns = dense.shape
    chunk = columns // TILE
    dense[...] = jnp.zeros(dense.shape, BF)

    def put(part, carried):
        target = pl.multiple_of(dst_ref[part] * TILE, TILE)
        origin = pl.multiple_of(lax.rem(part, chunk) * TILE, TILE)
        dense[lax.div(part, chunk), pl.ds(target, TILE), pl.ds(origin, TILE)] = cut_ref[part]
        return carried

    lax.fori_loop(0, chunks * chunk, put, 0)
    copy = pltpu.make_async_copy(dense, dense_hbm, sem)
    copy.start()
    copy.wait()


def pair_kernel(half_ref, own_ref, other_ref, pair_ref):
    rows = own_ref.shape[0]
    place = pl.multiple_of(half_ref[0] * rows, TILE)
    pair_ref[pl.ds(place, rows)] = own_ref[...]
    pair_ref[pl.ds(pl.multiple_of(rows - place, TILE), rows)] = other_ref[...]


def cut_sum_kernel(cut_hbm, far_hbm, total_ref, cut, far, sems):
    chunks = cut.shape[0]
    chunk = far.shape[0] // chunks
    width = far.shape[2]
    copies = []
    for piece in range(chunks):
        span = pl.ds(piece * chunk, chunk)
        copies.append(
            (
                pltpu.make_async_copy(cut_hbm.at[piece], cut.at[piece], sems.at[piece]),
                pltpu.make_async_copy(far_hbm.at[span], far.at[span], sems.at[chunks + piece]),
            )
        )
    for pair in copies:
        for copy in pair:
            copy.start()
    for piece in range(chunks):
        for copy in copies[piece]:
            copy.wait()
        arrived = far[pl.ds(piece * chunk, chunk)].reshape(chunk * TILE, width)
        term = product(cut[piece], arrived)
        total_ref[...] = term if piece == 0 else total_ref[...] + term


def middle_kernel(
    sum_ref,
    cut_sum_ref,
    last_ref,
    bias_ref,
    cotangent_ref,
    far_mat_ref,
    near_mat_ref,
    left_mat_ref,
    right_mat_ref,
    cut_hbm,
    hidden_ref,
    grad_ref,
    left_hbm,
    right_hbm,
    left_term_hbm,
    right_term_hbm,
    terms_hbm,
    messages,
    nexts,
    cut,
    terms,
    sems,
):
    chunks = cut.shape[0]
    chunk = terms.shape[0] // chunks
    loads = [
        pltpu.make_async_copy(cut_hbm.at[piece], cut.at[piece], sems.at[piece])
        for piece in range(chunks)
    ]
    for copy in loads:
        copy.start()
    total = sum_ref[...] + cut_sum_ref[...] + product(far_mat_ref[...], last_ref[...])
    activated, derivative = silu_parts(total + bias_ref[...])
    hidden_ref[...] = activated.astype(BF)
    grad = (cotangent_ref[...].astype(F32) * derivative).T.astype(BF)
    grad_ref[...] = grad
    stores = []
    for place, (mat_ref, out_hbm) in enumerate(
        ((far_mat_ref, left_hbm), (near_mat_ref, right_hbm))
    ):
        messages[place] = product(grad, mat_ref[...]).astype(BF)
        stores.append(
            pltpu.make_async_copy(messages.at[place], out_hbm, sems.at[2 * chunks + place])
        )
        stores[-1].start()
    for place, (mat_ref, out_hbm) in enumerate(
        ((left_mat_ref, left_term_hbm), (right_mat_ref, right_term_hbm))
    ):
        nexts[place] = product(grad, mat_ref[...])
        stores.append(
            pltpu.make_async_copy(nexts.at[place], out_hbm, sems.at[2 * chunks + 2 + place])
        )
        stores[-1].start()
    for piece in range(chunks):
        loads[piece].wait()
        result = product(grad, cut[piece]).astype(BF)
        for slot in range(chunk):
            terms[piece * chunk + slot] = result[:, slot * TILE : (slot + 1) * TILE]
        span = pl.ds(piece * chunk, chunk)
        stores.append(
            pltpu.make_async_copy(terms.at[span], terms_hbm.at[span], sems.at[chunks + piece])
        )
        stores[-1].start()
    for copy in stores:
        copy.wait()


def gather_kernel(blk_ref, live_ref, arrived_ref, total_ref):
    total_ref[...] = jnp.zeros(total_ref.shape, F32)

    def add(part, carried):
        @pl.when(live_ref[part] > 0)
        def _():
            columns = pl.ds(pl.multiple_of(blk_ref[part] * TILE, TILE), TILE)
            total_ref[:, columns] += arrived_ref[part].astype(F32)

        return carried

    lax.fori_loop(0, arrived_ref.shape[0], add, 0)


def hop_kernel(grad_ref, mat_ref, arrived_ref, out_ref):
    term = product(grad_ref[...], mat_ref[...]) + arrived_ref[...].astype(F32)
    out_ref[...] = term.astype(BF)


def close_kernel(half_ref, grad_ref, mat_ref, left_ref, right_ref, own_ref, other_ref):
    rows = grad_ref.shape[1]
    mine = pl.ds(pl.multiple_of(half_ref[0] * rows, TILE), rows)
    theirs = pl.ds(pl.multiple_of((1 - half_ref[0]) * rows, TILE), rows)

    def total(columns):
        arrived = left_ref[:, columns].astype(F32) + right_ref[:, columns].astype(F32)
        return product(grad_ref[...], mat_ref[:, columns]) + arrived

    other_ref[...] = total(theirs).astype(BF)
    own_ref[...] = total(mine)


def last_kernel(own_ref, other_ref, cut_ref, weight_ref, out_ref):
    total = own_ref[...] + other_ref[...].astype(F32) + cut_ref[...]
    out_ref[...] = lax.dot_general(
        total.T.astype(BF), weight_ref[...], (((1,), (1,)), ((), ())), preferred_element_type=F32
    ).astype(BF)


def on_device(
    features,
    weight,
    bias,
    cotangent,
    in_tiles,
    in_pos,
    in_count,
    cut_tiles,
    send_blk,
    send_live,
    recv_dst,
):
    rows, width = features.shape
    blocks = rows // TILE
    peers = lax.axis_size("blk")
    parts = lax.axis_size("dom")
    ring = peers // FAR
    reach = ring // 2
    me = lax.axis_index("blk")
    place, half = me % ring, me // ring
    wide = FAR * rows
    chunks = min(CHUNKS, parts)
    send_to, is_live, dst = send_blk[0, 0], send_live[0, 0], recv_dst[0, 0]
    shape = jax.ShapeDtypeStruct

    def along_ring(value, by):
        moves = [
            (side * ring + spot, side * ring + (spot + by) % ring)
            for side in range(FAR)
            for spot in range(ring)
        ]
        return lax.ppermute(value, "blk", moves)

    def across(value):
        return lax.ppermute(value, "blk", [(i, (i + ring) % peers) for i in range(peers)])

    projected, outgoing = call(
        project_kernel,
        "project",
        (shape((rows, width), BF), pltpu.HBM((parts, TILE, width), BF)),
        [HBM] * 4,
        (VMEM, HBM),
        [
            pltpu.SMEM((parts,), jnp.int32),
            pltpu.SMEM((parts,), jnp.int32),
            pltpu.VMEM(features.shape, BF),
            pltpu.VMEM(weight.shape, BF),
            pltpu.VMEM((TILE, width), BF),
            pltpu.SemaphoreType.DMA((4,)),
            pltpu.SemaphoreType.DMA((parts,)),
        ],
    )(in_hbm(send_to), in_hbm(is_live), in_hbm(features), in_hbm(weight))
    partner = across(projected)
    incoming = lax.all_to_all(outgoing, "dom", split_axis=0, concat_axis=0, tiled=True)

    dense = call(
        lambda *refs: spread_kernel(ring, blocks, *refs),
        "spread",
        tuple([shape((rows, wide), BF)] * ring),
        [SMEM, SMEM, SMEM, VMEM],
        tuple([VMEM] * ring),
        moved=10 << 20,
    )(in_pos[0, 0].reshape(-1), in_count[0, 0], place.reshape(1), in_tiles[0, 0])
    dense_cut = call(
        spread_cut_kernel,
        "spread_cut",
        pltpu.HBM((chunks, rows, parts // chunks * TILE), BF),
        [SMEM, VMEM],
        HBM,
        [
            pltpu.VMEM((chunks, rows, parts // chunks * TILE), BF),
            pltpu.SemaphoreType.DMA,
        ],
        moved=6 << 20,
    )(dst, cut_tiles[0, 0])

    pair = call(
        pair_kernel, "pair", shape((wide, width), BF), [SMEM, VMEM, VMEM], VMEM, flops=PAIR_COST
    )(half.reshape(1), projected, partner)
    running = product(dense[0], pair)
    right = left = pair
    for hop in range(1, reach):
        right, left = along_ring(right, 1), along_ring(left, -1)
        running = running + product(dense[ring - hop], right)
        running = running + product(dense[hop], left)
    left = along_ring(left, -1)
    cut_sum = call(
        cut_sum_kernel,
        "cut_sum",
        shape((rows, width), F32),
        [HBM, HBM],
        VMEM,
        [
            pltpu.VMEM(dense_cut.shape, BF),
            pltpu.VMEM((parts, TILE, width), BF),
            pltpu.SemaphoreType.DMA((2 * chunks,)),
        ],
        flops=CUT_COST,
    )(in_hbm(dense_cut), in_hbm(incoming))

    hidden, grad_pre, left, right, left_term, right_term, terms = call(
        middle_kernel,
        "middle",
        (shape((rows, width), BF), shape((width, rows), BF))
        + (pltpu.HBM((width, wide), BF),) * 2
        + (pltpu.HBM((width, wide), F32),) * 2
        + (pltpu.HBM((parts, width, TILE), BF),),
        [VMEM] * 9 + [HBM],
        (VMEM,) * 2 + (HBM,) * 5,
        [
            pltpu.VMEM((2, width, wide), BF),
            pltpu.VMEM((2, width, wide), F32),
            pltpu.VMEM(dense_cut.shape, BF),
            pltpu.VMEM((parts, width, TILE), BF),
            pltpu.SemaphoreType.DMA((2 * chunks + 4,)),
        ],
    )(
        running,
        cut_sum,
        left,
        bias.reshape(1, width),
        cotangent,
        dense[reach],
        dense[reach - 1],
        dense[ring - reach + 1],
        dense[reach - 2],
        in_hbm(dense_cut),
    )

    def add_on(mat, arrived):
        return call(hop_kernel, "hop", shape((width, wide), BF), [VMEM] * 3, VMEM)(
            grad_pre, mat, arrived
        )

    def plus(term, arrived):
        return (term + arrived.astype(F32)).astype(BF)

    left, right = along_ring(left, -1), along_ring(right, 1)
    returned = lax.all_to_all(terms, "dom", split_axis=0, concat_axis=0, tiled=True)
    for hop in range(reach - 1, 0, -1):
        if hop == reach - 1:
            left = plus(left_term, left)
            if hop > 1:
                right = plus(right_term, right)
        else:
            left = add_on(dense[ring - hop], left)
            if hop > 1:
                right = add_on(dense[hop - 1], right)
        left = along_ring(left, -1)
        if hop > 1:
            right = along_ring(right, 1)
    own, other = call(
        close_kernel,
        "close",
        (shape((width, rows), F32), shape((width, rows), BF)),
        [SMEM] + [VMEM] * 4,
        (VMEM, VMEM),
        flops=CLOSE_COST,
    )(half.reshape(1), grad_pre, dense[0], right, left)
    other = across(other)
    from_cuts = call(
        gather_kernel, "gather", shape((width, rows), F32), [SMEM, SMEM, VMEM], VMEM, moved=2 << 20
    )(send_to, is_live, returned)
    grad_features = call(
        last_kernel, "last", shape((rows, width), BF), [VMEM] * 4, VMEM
    )(own, other, from_cuts, weight)
    return (hidden, grad_features)


def solution(mesh):
    in_specs = (
        P(("dom", "blk"), None),
        P(),
        P(),
        P(("dom", "blk"), None),
        P("dom", "blk", None, None, None, None),
        P("dom", "blk", None, None),
        P("dom", "blk", None),
        P("dom", "blk", None, None, None),
        P("dom", "blk", None),
        P("dom", "blk", None),
        P("dom", "blk", None),
    )
    out_specs = (P(("dom", "blk"), None), P(("dom", "blk"), None))
    return jax.shard_map(
        on_device, mesh=mesh, in_specs=in_specs, out_specs=out_specs, check_vma=False
    )
```

```python
import jax
import jax.numpy as jnp
from jax import lax
from jax.experimental import pallas as pl
from jax.experimental.pallas import tpu as pltpu
from jax.sharding import PartitionSpec as P

BF, F32 = jnp.bfloat16, jnp.float32
TILE = 128
FAR = 2
CHUNKS = 8
VMEM_LIMIT = 16 * 1024 * 1024
PAIR_COST = 100_000_000_000
CLOSE_COST = 30_000_000_000
CUT_COST = 2_000_000_000


def spec(space):
    return pl.BlockSpec(memory_space=space)


SMEM, VMEM, HBM = spec(pltpu.SMEM), spec(pltpu.VMEM), spec(pltpu.HBM)


def call(kernel, name, out_shape, in_specs, out_specs, scratch=(), flops=0, moved=0):
    return pl.pallas_call(
        kernel,
        out_shape=out_shape,
        in_specs=in_specs,
        out_specs=out_specs,
        scratch_shapes=scratch,
        compiler_params=pltpu.CompilerParams(vmem_limit_bytes=VMEM_LIMIT),
        cost_estimate=pl.CostEstimate(flops=flops, bytes_accessed=moved, transcendentals=0),
        name=name,
    )


def in_hbm(value):
    return pltpu.with_memory_space_constraint(value, pltpu.HBM)


def product(left, right):
    return jnp.dot(left, right, preferred_element_type=F32)


def silu_parts(preact):
    sigmoid = 1.0 / (1.0 + jnp.exp(-preact))
    return (preact * sigmoid, sigmoid * (1.0 + preact * (1.0 - sigmoid)))


def project_kernel(features_hbm, weight_hbm, projected_ref, features, weight, sems):
    copies = [
        pltpu.make_async_copy(features_hbm, features, sems.at[0]),
        pltpu.make_async_copy(weight_hbm, weight, sems.at[1]),
    ]
    for copy in copies:
        copy.start()
    for copy in copies:
        copy.wait()
    projected_ref[...] = product(features[...], weight[...]).astype(BF)


def fill_kernel(
    blk_hbm, live_hbm, projected_ref, outgoing_hbm, blk_ref, live_ref, zeros, load_sems, sems
):
    parts = outgoing_hbm.shape[0]
    loads = [
        pltpu.make_async_copy(blk_hbm, blk_ref, load_sems.at[0]),
        pltpu.make_async_copy(live_hbm, live_ref, load_sems.at[1]),
    ]
    for copy in loads:
        copy.start()
    zeros[...] = jnp.zeros(zeros.shape, BF)
    for copy in loads:
        copy.wait()

    def start(part, carried):
        @pl.when(live_ref[part] > 0)
        def _():
            row = pl.multiple_of(blk_ref[part] * TILE, TILE)
            pltpu.make_async_copy(
                projected_ref.at[pl.ds(row, TILE)], outgoing_hbm.at[part], sems.at[part]
            ).start()

        @pl.when(live_ref[part] <= 0)
        def _():
            pltpu.make_async_copy(zeros, outgoing_hbm.at[part], sems.at[part]).start()

        return carried

    def wait(part, carried):
        pltpu.make_async_copy(zeros, outgoing_hbm.at[part], sems.at[part]).wait()
        return carried

    lax.fori_loop(0, parts, start, 0)
    lax.fori_loop(0, parts, wait, 0)


def spread_kernel(ring, blocks, pos_ref, count_ref, place_ref, tiles_ref, *outs):
    rows = blocks * TILE
    place = place_ref[0]
    for offset in range(ring):
        dense = outs[offset]
        dense[...] = jnp.zeros(dense.shape, BF)
        spot = lax.rem(place + offset, ring)
        for half in range(FAR):
            source = half * ring + spot

            def put(slot, carried, dense=dense, half=half, source=source):
                position = pos_ref[source * tiles_ref.shape[1] + slot]
                target = pl.multiple_of(position // blocks * TILE, TILE)
                origin = pl.multiple_of(half * rows + position % blocks * TILE, TILE)
                dense[pl.ds(target, TILE), pl.ds(origin, TILE)] = tiles_ref[source, slot]
                return carried

            lax.fori_loop(0, count_ref[source], put, 0)


def spread_cut_kernel(dst_ref, cut_ref, dense_hbm, dense, sem):
    chunks, _, columns = dense.shape
    chunk = columns // TILE
    dense[...] = jnp.zeros(dense.shape, BF)

    def put(part, carried):
        target = pl.multiple_of(dst_ref[part] * TILE, TILE)
        origin = pl.multiple_of(lax.rem(part, chunk) * TILE, TILE)
        dense[lax.div(part, chunk), pl.ds(target, TILE), pl.ds(origin, TILE)] = cut_ref[part]
        return carried

    lax.fori_loop(0, chunks * chunk, put, 0)
    copy = pltpu.make_async_copy(dense, dense_hbm, sem)
    copy.start()
    copy.wait()


def pair_kernel(half_ref, own_ref, other_ref, pair_ref):
    rows = own_ref.shape[0]
    place = pl.multiple_of(half_ref[0] * rows, TILE)
    pair_ref[pl.ds(place, rows)] = own_ref[...]
    pair_ref[pl.ds(pl.multiple_of(rows - place, TILE), rows)] = other_ref[...]


def cut_sum_kernel(cut_hbm, far_hbm, total_ref, cut, far, sems):
    chunks = cut.shape[0]
    chunk = far.shape[0] // chunks
    width = far.shape[2]
    copies = []
    for piece in range(chunks):
        span = pl.ds(piece * chunk, chunk)
        copies.append(
            (
                pltpu.make_async_copy(cut_hbm.at[piece], cut.at[piece], sems.at[piece]),
                pltpu.make_async_copy(far_hbm.at[span], far.at[span], sems.at[chunks + piece]),
            )
        )
    for pair in copies:
        for copy in pair:
            copy.start()
    for piece in range(chunks):
        for copy in copies[piece]:
            copy.wait()
        arrived = far[pl.ds(piece * chunk, chunk)].reshape(chunk * TILE, width)
        term = product(cut[piece], arrived)
        total_ref[...] = term if piece == 0 else total_ref[...] + term


def middle_kernel(
    sum_ref,
    cut_sum_ref,
    last_ref,
    bias_ref,
    cotangent_ref,
    far_mat_ref,
    near_mat_ref,
    cut_hbm,
    hidden_ref,
    grad_ref,
    left_hbm,
    right_hbm,
    terms_hbm,
    messages,
    cut,
    terms,
    sems,
):
    chunks = cut.shape[0]
    chunk = terms.shape[0] // chunks
    loads = [
        pltpu.make_async_copy(cut_hbm.at[piece], cut.at[piece], sems.at[piece])
        for piece in range(chunks)
    ]
    for copy in loads:
        copy.start()
    total = sum_ref[...] + cut_sum_ref[...] + product(far_mat_ref[...], last_ref[...])
    activated, derivative = silu_parts(total + bias_ref[...])
    hidden_ref[...] = activated.astype(BF)
    grad = (cotangent_ref[...].astype(F32) * derivative).T.astype(BF)
    grad_ref[...] = grad
    stores = []
    for place, (mat_ref, out_hbm) in enumerate(
        ((far_mat_ref, left_hbm), (near_mat_ref, right_hbm))
    ):
        messages[place] = product(grad, mat_ref[...]).astype(BF)
        stores.append(
            pltpu.make_async_copy(messages.at[place], out_hbm, sems.at[2 * chunks + place])
        )
        stores[-1].start()
    for piece in range(chunks):
        loads[piece].wait()
        result = product(grad, cut[piece]).astype(BF)
        for slot in range(chunk):
            terms[piece * chunk + slot] = result[:, slot * TILE : (slot + 1) * TILE]
        span = pl.ds(piece * chunk, chunk)
        stores.append(
            pltpu.make_async_copy(terms.at[span], terms_hbm.at[span], sems.at[chunks + piece])
        )
        stores[-1].start()
    for copy in stores:
        copy.wait()


def gather_kernel(blk_ref, live_ref, arrived_ref, total_ref):
    total_ref[...] = jnp.zeros(total_ref.shape, F32)

    def add(part, carried):
        @pl.when(live_ref[part] > 0)
        def _():
            columns = pl.ds(pl.multiple_of(blk_ref[part] * TILE, TILE), TILE)
            total_ref[:, columns] += arrived_ref[part].astype(F32)

        return carried

    lax.fori_loop(0, arrived_ref.shape[0], add, 0)


def hop_kernel(grad_ref, mat_ref, arrived_ref, out_ref):
    term = product(grad_ref[...], mat_ref[...]) + arrived_ref[...].astype(F32)
    out_ref[...] = term.astype(BF)


def halves(half_ref, rows):
    mine = pl.ds(pl.multiple_of(half_ref[0] * rows, TILE), rows)
    theirs = pl.ds(pl.multiple_of((1 - half_ref[0]) * rows, TILE), rows)
    return mine, theirs


def last_hop_kernel(half_ref, grad_ref, mat_ref, arrived_ref, own_ref, other_ref):
    mine, theirs = halves(half_ref, grad_ref.shape[1])
    for columns, out_ref in ((theirs, other_ref), (mine, own_ref)):
        term = product(grad_ref[...], mat_ref[:, columns]) + arrived_ref[:, columns].astype(F32)
        out_ref[...] = term.astype(BF)


def own_place_kernel(half_ref, grad_ref, mat_ref, own_ref, other_ref):
    mine, theirs = halves(half_ref, grad_ref.shape[1])
    other_ref[...] = product(grad_ref[...], mat_ref[:, theirs]).astype(BF)
    own_ref[...] = product(grad_ref[...], mat_ref[:, mine])


def last_kernel(own_ref, *refs):
    *arrived_refs, cut_ref, weight_ref, out_ref = refs
    total = own_ref[...] + cut_ref[...]
    for arrived_ref in arrived_refs:
        total += arrived_ref[...].astype(F32)
    out_ref[...] = lax.dot_general(
        total.T.astype(BF), weight_ref[...], (((1,), (1,)), ((), ())), preferred_element_type=F32
    ).astype(BF)


def on_device(
    features,
    weight,
    bias,
    cotangent,
    in_tiles,
    in_pos,
    in_count,
    cut_tiles,
    send_blk,
    send_live,
    recv_dst,
):
    rows, width = features.shape
    blocks = rows // TILE
    peers = lax.axis_size("blk")
    parts = lax.axis_size("dom")
    ring = peers // FAR
    reach = ring // 2
    me = lax.axis_index("blk")
    place, half = me % ring, me // ring
    wide = FAR * rows
    chunks = min(CHUNKS, parts)
    send_to, is_live, dst = send_blk[0, 0], send_live[0, 0], recv_dst[0, 0]
    shape = jax.ShapeDtypeStruct

    def along_ring(value, by):
        moves = [
            (side * ring + spot, side * ring + (spot + by) % ring)
            for side in range(FAR)
            for spot in range(ring)
        ]
        return lax.ppermute(value, "blk", moves)

    def across_and_along(value, by):
        moves = [
            (
                side * ring + spot,
                (side + 1) % FAR * ring + (spot + by) % ring,
            )
            for side in range(FAR)
            for spot in range(ring)
        ]
        return lax.ppermute(value, "blk", moves)

    def across(value):
        return lax.ppermute(value, "blk", [(i, (i + ring) % peers) for i in range(peers)])

    projected = call(
        project_kernel,
        "project",
        shape((rows, width), BF),
        [HBM, HBM],
        VMEM,
        [
            pltpu.VMEM(features.shape, BF),
            pltpu.VMEM(weight.shape, BF),
            pltpu.SemaphoreType.DMA((2,)),
        ],
    )(in_hbm(features), in_hbm(weight))
    partner = across(projected)
    outgoing = call(
        fill_kernel,
        "fill",
        pltpu.HBM((parts, TILE, width), BF),
        [HBM, HBM, VMEM],
        HBM,
        [
            pltpu.SMEM((parts,), jnp.int32),
            pltpu.SMEM((parts,), jnp.int32),
            pltpu.VMEM((TILE, width), BF),
            pltpu.SemaphoreType.DMA((2,)),
            pltpu.SemaphoreType.DMA((parts,)),
        ],
    )(in_hbm(send_to), in_hbm(is_live), projected)
    incoming = lax.all_to_all(outgoing, "dom", split_axis=0, concat_axis=0, tiled=True)

    dense = call(
        lambda *refs: spread_kernel(ring, blocks, *refs),
        "spread",
        tuple([shape((rows, wide), BF)] * ring),
        [SMEM, SMEM, SMEM, VMEM],
        tuple([VMEM] * ring),
        moved=10 << 20,
    )(in_pos[0, 0].reshape(-1), in_count[0, 0], place.reshape(1), in_tiles[0, 0])
    dense_cut = call(
        spread_cut_kernel,
        "spread_cut",
        pltpu.HBM((chunks, rows, parts // chunks * TILE), BF),
        [SMEM, VMEM],
        HBM,
        [
            pltpu.VMEM((chunks, rows, parts // chunks * TILE), BF),
            pltpu.SemaphoreType.DMA,
        ],
        moved=6 << 20,
    )(dst, cut_tiles[0, 0])

    pair = call(
        pair_kernel, "pair", shape((wide, width), BF), [SMEM, VMEM, VMEM], VMEM, flops=PAIR_COST
    )(half.reshape(1), projected, partner)
    running = product(dense[0], pair)
    right = left = pair
    for hop in range(1, reach):
        right, left = along_ring(right, 1), along_ring(left, -1)
        running = running + product(dense[ring - hop], right)
        running = running + product(dense[hop], left)
    left = along_ring(left, -1)
    cut_sum = call(
        cut_sum_kernel,
        "cut_sum",
        shape((rows, width), F32),
        [HBM, HBM],
        VMEM,
        [
            pltpu.VMEM(dense_cut.shape, BF),
            pltpu.VMEM((parts, TILE, width), BF),
            pltpu.SemaphoreType.DMA((2 * chunks,)),
        ],
        flops=CUT_COST,
    )(in_hbm(dense_cut), in_hbm(incoming))

    hidden, grad_pre, left, right, terms = call(
        middle_kernel,
        "middle",
        (shape((rows, width), BF), shape((width, rows), BF))
        + (pltpu.HBM((width, wide), BF),) * 2
        + (pltpu.HBM((parts, width, TILE), BF),),
        [VMEM] * 7 + [HBM],
        (VMEM,) * 2 + (HBM,) * 3,
        [
            pltpu.VMEM((2, width, wide), BF),
            pltpu.VMEM(dense_cut.shape, BF),
            pltpu.VMEM((parts, width, TILE), BF),
            pltpu.SemaphoreType.DMA((2 * chunks + 2,)),
        ],
    )(
        running,
        cut_sum,
        left,
        bias.reshape(1, width),
        cotangent,
        dense[reach],
        dense[reach - 1],
        in_hbm(dense_cut),
    )

    def add_on(mat, arrived):
        return call(hop_kernel, "hop", shape((width, wide), BF), [VMEM] * 3, VMEM)(
            grad_pre, mat, arrived
        )

    left, right = along_ring(left, -1), along_ring(right, 1)
    returned = lax.all_to_all(terms, "dom", split_axis=0, concat_axis=0, tiled=True)
    own_half = half.reshape(1)

    def deliver(mat, arrived, by, flops):
        own, other = call(
            last_hop_kernel,
            "last_hop",
            (shape((width, rows), BF),) * 2,
            [SMEM] + [VMEM] * 3,
            (VMEM, VMEM),
            flops=flops,
        )(own_half, grad_pre, mat, arrived)
        return across_and_along(other, by), along_ring(own, by)

    own, other = call(
        own_place_kernel,
        "own_place",
        (shape((width, rows), F32), shape((width, rows), BF)),
        [SMEM] + [VMEM] * 2,
        (VMEM, VMEM),
    )(own_half, grad_pre, dense[0])
    arrived = (across(other),)
    for hop in range(reach - 1, 0, -1):
        if hop > 1:
            left = along_ring(add_on(dense[ring - hop], left), -1)
        else:
            arrived += deliver(dense[ring - hop], left, -1, CLOSE_COST)
        if hop > 2:
            right = along_ring(add_on(dense[hop - 1], right), 1)
        elif hop == 2:
            arrived += deliver(dense[hop - 1], right, 1, 0)
    from_cuts = call(
        gather_kernel, "gather", shape((width, rows), F32), [SMEM, SMEM, VMEM], VMEM, moved=2 << 20
    )(send_to, is_live, returned)
    grad_features = call(
        last_kernel, "last", shape((rows, width), BF), [VMEM] * (3 + len(arrived)), VMEM
    )(own, *arrived, from_cuts, weight)
    return (hidden, grad_features)


def solution(mesh):
    in_specs = (
        P(("dom", "blk"), None),
        P(),
        P(),
        P(("dom", "blk"), None),
        P("dom", "blk", None, None, None, None),
        P("dom", "blk", None, None),
        P("dom", "blk", None),
        P("dom", "blk", None, None, None),
        P("dom", "blk", None),
        P("dom", "blk", None),
        P("dom", "blk", None),
    )
    out_specs = (P(("dom", "blk"), None), P(("dom", "blk"), None))
    return jax.shard_map(
        on_device, mesh=mesh, in_specs=in_specs, out_specs=out_specs, check_vma=False
    )
```

```python
import jax
import jax.numpy as jnp
from jax import lax
from jax.experimental import pallas as pl
from jax.experimental.pallas import tpu as pltpu
from jax.sharding import PartitionSpec as P

BF, F32 = jnp.bfloat16, jnp.float32
TILE = 128
FAR = 2
CHUNKS = 8
VMEM_LIMIT = 16 * 1024 * 1024
PAIR_COST = 100_000_000_000
CLOSE_COST = 30_000_000_000
CUT_COST = 2_000_000_000
COLLECT_COST = 2_000_000


def spec(space):
    return pl.BlockSpec(memory_space=space)


SMEM, VMEM, HBM = spec(pltpu.SMEM), spec(pltpu.VMEM), spec(pltpu.HBM)


def call(kernel, name, out_shape, in_specs, out_specs, scratch=(), flops=0, moved=0):
    return pl.pallas_call(
        kernel,
        out_shape=out_shape,
        in_specs=in_specs,
        out_specs=out_specs,
        scratch_shapes=scratch,
        compiler_params=pltpu.CompilerParams(vmem_limit_bytes=VMEM_LIMIT),
        cost_estimate=pl.CostEstimate(flops=flops, bytes_accessed=moved, transcendentals=0),
        name=name,
    )


def in_hbm(value):
    return pltpu.with_memory_space_constraint(value, pltpu.HBM)


def product(left, right):
    return jnp.dot(left, right, preferred_element_type=F32)


def silu_parts(preact):
    sigmoid = 1.0 / (1.0 + jnp.exp(-preact))
    return (preact * sigmoid, sigmoid * (1.0 + preact * (1.0 - sigmoid)))


def project_kernel(features_hbm, weight_hbm, projected_ref, features, weight, sems):
    copies = [
        pltpu.make_async_copy(features_hbm, features, sems.at[0]),
        pltpu.make_async_copy(weight_hbm, weight, sems.at[1]),
    ]
    for copy in copies:
        copy.start()
    for copy in copies:
        copy.wait()
    projected_ref[...] = product(features[...], weight[...]).astype(BF)


def fill_kernel(
    blk_hbm, live_hbm, projected_ref, outgoing_hbm, blk_ref, live_ref, zeros, load_sems, sems
):
    parts = outgoing_hbm.shape[0]
    loads = [
        pltpu.make_async_copy(blk_hbm, blk_ref, load_sems.at[0]),
        pltpu.make_async_copy(live_hbm, live_ref, load_sems.at[1]),
    ]
    for copy in loads:
        copy.start()
    zeros[...] = jnp.zeros(zeros.shape, BF)
    for copy in loads:
        copy.wait()

    def start(part, carried):
        @pl.when(live_ref[part] > 0)
        def _():
            row = pl.multiple_of(blk_ref[part] * TILE, TILE)
            pltpu.make_async_copy(
                projected_ref.at[pl.ds(row, TILE)], outgoing_hbm.at[part], sems.at[part]
            ).start()

        @pl.when(live_ref[part] <= 0)
        def _():
            pltpu.make_async_copy(zeros, outgoing_hbm.at[part], sems.at[part]).start()

        return carried

    def wait(part, carried):
        pltpu.make_async_copy(zeros, outgoing_hbm.at[part], sems.at[part]).wait()
        return carried

    lax.fori_loop(0, parts, start, 0)
    lax.fori_loop(0, parts, wait, 0)


def spread_kernel(ring, blocks, pos_ref, count_ref, place_ref, tiles_ref, *outs):
    rows = blocks * TILE
    place = place_ref[0]
    for offset in range(ring):
        dense = outs[offset]
        dense[...] = jnp.zeros(dense.shape, BF)
        spot = lax.rem(place + offset, ring)
        for half in range(FAR):
            source = half * ring + spot

            def put(slot, carried, dense=dense, half=half, source=source):
                position = pos_ref[source * tiles_ref.shape[1] + slot]
                target = pl.multiple_of(position // blocks * TILE, TILE)
                origin = pl.multiple_of(half * rows + position % blocks * TILE, TILE)
                dense[pl.ds(target, TILE), pl.ds(origin, TILE)] = tiles_ref[source, slot]
                return carried

            lax.fori_loop(0, count_ref[source], put, 0)


def spread_cut_kernel(dst_ref, cut_ref, dense_hbm, dense, sem):
    chunks, _, columns = dense.shape
    chunk = columns // TILE
    dense[...] = jnp.zeros(dense.shape, BF)

    def put(part, carried):
        target = pl.multiple_of(dst_ref[part] * TILE, TILE)
        origin = pl.multiple_of(lax.rem(part, chunk) * TILE, TILE)
        dense[lax.div(part, chunk), pl.ds(target, TILE), pl.ds(origin, TILE)] = cut_ref[part]
        return carried

    lax.fori_loop(0, chunks * chunk, put, 0)
    copy = pltpu.make_async_copy(dense, dense_hbm, sem)
    copy.start()
    copy.wait()


def pair_kernel(half_ref, own_ref, other_ref, pair_ref):
    rows = own_ref.shape[0]
    place = pl.multiple_of(half_ref[0] * rows, TILE)
    pair_ref[pl.ds(place, rows)] = own_ref[...]
    pair_ref[pl.ds(pl.multiple_of(rows - place, TILE), rows)] = other_ref[...]


def cut_sum_kernel(cut_hbm, far_hbm, total_ref, cut, far, sems):
    chunks = cut.shape[0]
    chunk = far.shape[0] // chunks
    width = far.shape[2]
    copies = []
    for piece in range(chunks):
        span = pl.ds(piece * chunk, chunk)
        copies.append(
            (
                pltpu.make_async_copy(cut_hbm.at[piece], cut.at[piece], sems.at[piece]),
                pltpu.make_async_copy(far_hbm.at[span], far.at[span], sems.at[chunks + piece]),
            )
        )
    for pair in copies:
        for copy in pair:
            copy.start()
    for piece in range(chunks):
        for copy in copies[piece]:
            copy.wait()
        arrived = far[pl.ds(piece * chunk, chunk)].reshape(chunk * TILE, width)
        term = product(cut[piece], arrived)
        total_ref[...] = term if piece == 0 else total_ref[...] + term


def middle_kernel(
    sum_ref,
    cut_sum_ref,
    last_ref,
    bias_ref,
    cotangent_ref,
    far_mat_ref,
    near_mat_ref,
    cut_hbm,
    hidden_ref,
    grad_ref,
    left_hbm,
    right_hbm,
    terms_hbm,
    messages,
    cut,
    terms,
    sems,
):
    chunks = cut.shape[0]
    chunk = terms.shape[0] // chunks
    loads = [
        pltpu.make_async_copy(cut_hbm.at[piece], cut.at[piece], sems.at[piece])
        for piece in range(chunks)
    ]
    for copy in loads:
        copy.start()
    total = sum_ref[...] + cut_sum_ref[...] + product(far_mat_ref[...], last_ref[...])
    activated, derivative = silu_parts(total + bias_ref[...])
    hidden_ref[...] = activated.astype(BF)
    grad = (cotangent_ref[...].astype(F32) * derivative).T.astype(BF)
    grad_ref[...] = grad
    stores = []
    for place, (mat_ref, out_hbm) in enumerate(
        ((far_mat_ref, left_hbm), (near_mat_ref, right_hbm))
    ):
        messages[place] = product(grad, mat_ref[...]).astype(BF)
        stores.append(
            pltpu.make_async_copy(messages.at[place], out_hbm, sems.at[2 * chunks + place])
        )
        stores[-1].start()
    for piece in range(chunks):
        loads[piece].wait()
        result = product(grad, cut[piece]).astype(BF)
        for slot in range(chunk):
            terms[piece * chunk + slot] = result[:, slot * TILE : (slot + 1) * TILE]
        span = pl.ds(piece * chunk, chunk)
        stores.append(
            pltpu.make_async_copy(terms.at[span], terms_hbm.at[span], sems.at[chunks + piece])
        )
        stores[-1].start()
    for copy in stores:
        copy.wait()


def hop_kernel(grad_ref, mat_ref, arrived_ref, out_ref):
    term = product(grad_ref[...], mat_ref[...]) + arrived_ref[...].astype(F32)
    out_ref[...] = term.astype(BF)


def halves(half_ref, rows):
    mine = pl.ds(pl.multiple_of(half_ref[0] * rows, TILE), rows)
    theirs = pl.ds(pl.multiple_of((1 - half_ref[0]) * rows, TILE), rows)
    return mine, theirs


def last_hop_kernel(half_ref, grad_ref, mat_ref, arrived_ref, own_ref, other_ref):
    mine, theirs = halves(half_ref, grad_ref.shape[1])
    for columns, out_ref in ((theirs, other_ref), (mine, own_ref)):
        term = product(grad_ref[...], mat_ref[:, columns]) + arrived_ref[:, columns].astype(F32)
        out_ref[...] = term.astype(BF)


def own_place_kernel(half_ref, grad_ref, mat_ref, own_ref, other_ref):
    mine, theirs = halves(half_ref, grad_ref.shape[1])
    other_ref[...] = product(grad_ref[...], mat_ref[:, theirs]).astype(BF)
    own_ref[...] = product(grad_ref[...], mat_ref[:, mine])


def collect_kernel(own_ref, *refs):
    *arrived_refs, total_ref = refs
    total = own_ref[...]
    for arrived_ref in arrived_refs:
        total += arrived_ref[...].astype(F32)
    total_ref[...] = total


def last_kernel(
    blk_ref, live_ref, terms_ref, sum_hbm, weight_hbm, out_ref, total, collected, weight, sems
):
    loads = [
        pltpu.make_async_copy(sum_hbm, collected, sems.at[0]),
        pltpu.make_async_copy(weight_hbm, weight, sems.at[1]),
    ]
    for copy in loads:
        copy.start()
    total[...] = jnp.zeros(total.shape, F32)

    def add(part, carried):
        @pl.when(live_ref[part] > 0)
        def _():
            columns = pl.ds(pl.multiple_of(blk_ref[part] * TILE, TILE), TILE)
            total[:, columns] += terms_ref[part].astype(F32)

        return carried

    lax.fori_loop(0, terms_ref.shape[0], add, 0)
    for copy in loads:
        copy.wait()
    rows = (total[...] + collected[...]).T.astype(BF)
    out_ref[...] = lax.dot_general(
        rows, weight[...], (((1,), (1,)), ((), ())), preferred_element_type=F32
    ).astype(BF)


def on_device(
    features,
    weight,
    bias,
    cotangent,
    in_tiles,
    in_pos,
    in_count,
    cut_tiles,
    send_blk,
    send_live,
    recv_dst,
):
    rows, width = features.shape
    blocks = rows // TILE
    peers = lax.axis_size("blk")
    parts = lax.axis_size("dom")
    ring = peers // FAR
    reach = ring // 2
    me = lax.axis_index("blk")
    place, half = me % ring, me // ring
    wide = FAR * rows
    chunks = min(CHUNKS, parts)
    send_to, is_live, dst = send_blk[0, 0], send_live[0, 0], recv_dst[0, 0]
    shape = jax.ShapeDtypeStruct

    def along_ring(value, by):
        moves = [
            (side * ring + spot, side * ring + (spot + by) % ring)
            for side in range(FAR)
            for spot in range(ring)
        ]
        return lax.ppermute(value, "blk", moves)

    def across_and_along(value, by):
        moves = [
            (
                side * ring + spot,
                (side + 1) % FAR * ring + (spot + by) % ring,
            )
            for side in range(FAR)
            for spot in range(ring)
        ]
        return lax.ppermute(value, "blk", moves)

    def across(value):
        return lax.ppermute(value, "blk", [(i, (i + ring) % peers) for i in range(peers)])

    projected = call(
        project_kernel,
        "project",
        shape((rows, width), BF),
        [HBM, HBM],
        VMEM,
        [
            pltpu.VMEM(features.shape, BF),
            pltpu.VMEM(weight.shape, BF),
            pltpu.SemaphoreType.DMA((2,)),
        ],
    )(in_hbm(features), in_hbm(weight))
    partner = across(projected)
    outgoing = call(
        fill_kernel,
        "fill",
        pltpu.HBM((parts, TILE, width), BF),
        [HBM, HBM, VMEM],
        HBM,
        [
            pltpu.SMEM((parts,), jnp.int32),
            pltpu.SMEM((parts,), jnp.int32),
            pltpu.VMEM((TILE, width), BF),
            pltpu.SemaphoreType.DMA((2,)),
            pltpu.SemaphoreType.DMA((parts,)),
        ],
    )(in_hbm(send_to), in_hbm(is_live), projected)
    incoming = lax.all_to_all(outgoing, "dom", split_axis=0, concat_axis=0, tiled=True)

    dense = call(
        lambda *refs: spread_kernel(ring, blocks, *refs),
        "spread",
        tuple([shape((rows, wide), BF)] * ring),
        [SMEM, SMEM, SMEM, VMEM],
        tuple([VMEM] * ring),
        moved=10 << 20,
    )(in_pos[0, 0].reshape(-1), in_count[0, 0], place.reshape(1), in_tiles[0, 0])
    dense_cut = call(
        spread_cut_kernel,
        "spread_cut",
        pltpu.HBM((chunks, rows, parts // chunks * TILE), BF),
        [SMEM, VMEM],
        HBM,
        [
            pltpu.VMEM((chunks, rows, parts // chunks * TILE), BF),
            pltpu.SemaphoreType.DMA,
        ],
        moved=6 << 20,
    )(dst, cut_tiles[0, 0])

    pair = call(
        pair_kernel, "pair", shape((wide, width), BF), [SMEM, VMEM, VMEM], VMEM, flops=PAIR_COST
    )(half.reshape(1), projected, partner)
    running = product(dense[0], pair)
    right = left = pair
    for hop in range(1, reach):
        right, left = along_ring(right, 1), along_ring(left, -1)
        running = running + product(dense[ring - hop], right)
        running = running + product(dense[hop], left)
    left = along_ring(left, -1)
    cut_sum = call(
        cut_sum_kernel,
        "cut_sum",
        shape((rows, width), F32),
        [HBM, HBM],
        VMEM,
        [
            pltpu.VMEM(dense_cut.shape, BF),
            pltpu.VMEM((parts, TILE, width), BF),
            pltpu.SemaphoreType.DMA((2 * chunks,)),
        ],
        flops=CUT_COST,
    )(in_hbm(dense_cut), in_hbm(incoming))

    hidden, grad_pre, left, right, terms = call(
        middle_kernel,
        "middle",
        (shape((rows, width), BF), shape((width, rows), BF))
        + (pltpu.HBM((width, wide), BF),) * 2
        + (pltpu.HBM((parts, width, TILE), BF),),
        [VMEM] * 7 + [HBM],
        (VMEM,) * 2 + (HBM,) * 3,
        [
            pltpu.VMEM((2, width, wide), BF),
            pltpu.VMEM(dense_cut.shape, BF),
            pltpu.VMEM((parts, width, TILE), BF),
            pltpu.SemaphoreType.DMA((2 * chunks + 2,)),
        ],
    )(
        running,
        cut_sum,
        left,
        bias.reshape(1, width),
        cotangent,
        dense[reach],
        dense[reach - 1],
        in_hbm(dense_cut),
    )

    def add_on(mat, arrived):
        return call(hop_kernel, "hop", shape((width, wide), BF), [VMEM] * 3, VMEM)(
            grad_pre, mat, arrived
        )

    left, right = along_ring(left, -1), along_ring(right, 1)
    returned = lax.all_to_all(terms, "dom", split_axis=0, concat_axis=0, tiled=True)
    own_half = half.reshape(1)

    def deliver(mat, arrived, by, flops):
        own, other = call(
            last_hop_kernel,
            "last_hop",
            (shape((width, rows), BF),) * 2,
            [SMEM] + [VMEM] * 3,
            (VMEM, VMEM),
            flops=flops,
        )(own_half, grad_pre, mat, arrived)
        return across_and_along(other, by), along_ring(own, by)

    own, other = call(
        own_place_kernel,
        "own_place",
        (shape((width, rows), F32), shape((width, rows), BF)),
        [SMEM] + [VMEM] * 2,
        (VMEM, VMEM),
    )(own_half, grad_pre, dense[0])
    arrived = (across(other),)
    for hop in range(reach - 1, 0, -1):
        if hop > 1:
            left = along_ring(add_on(dense[ring - hop], left), -1)
        else:
            arrived += deliver(dense[ring - hop], left, -1, CLOSE_COST)
        if hop > 2:
            right = along_ring(add_on(dense[hop - 1], right), 1)
        elif hop == 2:
            arrived += deliver(dense[hop - 1], right, 1, 0)
    collected = call(
        collect_kernel,
        "collect",
        shape((width, rows), F32),
        [VMEM] * (1 + len(arrived)),
        VMEM,
        flops=COLLECT_COST,
    )(own, *arrived)
    grad_features = call(
        last_kernel,
        "last",
        shape((rows, width), BF),
        [SMEM, SMEM, VMEM, HBM, HBM],
        VMEM,
        [
            pltpu.VMEM((width, rows), F32),
            pltpu.VMEM((width, rows), F32),
            pltpu.VMEM(weight.shape, BF),
            pltpu.SemaphoreType.DMA((2,)),
        ],
    )(send_to, is_live, returned, in_hbm(collected), in_hbm(weight))
    return (hidden, grad_features)


def solution(mesh):
    in_specs = (
        P(("dom", "blk"), None),
        P(),
        P(),
        P(("dom", "blk"), None),
        P("dom", "blk", None, None, None, None),
        P("dom", "blk", None, None),
        P("dom", "blk", None),
        P("dom", "blk", None, None, None),
        P("dom", "blk", None),
        P("dom", "blk", None),
        P("dom", "blk", None),
    )
    out_specs = (P(("dom", "blk"), None), P(("dom", "blk"), None))
    return jax.shard_map(
        on_device, mesh=mesh, in_specs=in_specs, out_specs=out_specs, check_vma=False
    )
```

```python
import jax
import jax.numpy as jnp
from jax import lax
from jax.experimental import pallas as pl
from jax.experimental.pallas import tpu as pltpu
from jax.sharding import PartitionSpec as P

BF, F32 = jnp.bfloat16, jnp.float32
TILE = 128
FAR = 2
CHUNKS = 8
VMEM_LIMIT = 16 * 1024 * 1024
PAIR_COST = 100_000_000_000
CLOSE_COST = 26_500_000_000
CUT_COST = 2_000_000_000


def spec(space):
    return pl.BlockSpec(memory_space=space)


SMEM, VMEM, HBM = spec(pltpu.SMEM), spec(pltpu.VMEM), spec(pltpu.HBM)


def call(kernel, name, out_shape, in_specs, out_specs, scratch=(), flops=0, moved=0):
    return pl.pallas_call(
        kernel,
        out_shape=out_shape,
        in_specs=in_specs,
        out_specs=out_specs,
        scratch_shapes=scratch,
        compiler_params=pltpu.CompilerParams(vmem_limit_bytes=VMEM_LIMIT),
        cost_estimate=pl.CostEstimate(flops=flops, bytes_accessed=moved, transcendentals=0),
        name=name,
    )


def in_hbm(value):
    return pltpu.with_memory_space_constraint(value, pltpu.HBM)


def product(left, right):
    return jnp.dot(left, right, preferred_element_type=F32)


def silu_parts(preact):
    sigmoid = 1.0 / (1.0 + jnp.exp(-preact))
    return (preact * sigmoid, sigmoid * (1.0 + preact * (1.0 - sigmoid)))


def project_kernel(features_hbm, weight_hbm, projected_ref, features, weight, sems):
    copies = [
        pltpu.make_async_copy(features_hbm, features, sems.at[0]),
        pltpu.make_async_copy(weight_hbm, weight, sems.at[1]),
    ]
    for copy in copies:
        copy.start()
    for copy in copies:
        copy.wait()
    projected_ref[...] = product(features[...], weight[...]).astype(BF)


def fill_kernel(
    blk_hbm, live_hbm, projected_ref, outgoing_hbm, blk_ref, live_ref, zeros, load_sems, sems
):
    parts = outgoing_hbm.shape[0]
    loads = [
        pltpu.make_async_copy(blk_hbm, blk_ref, load_sems.at[0]),
        pltpu.make_async_copy(live_hbm, live_ref, load_sems.at[1]),
    ]
    for copy in loads:
        copy.start()
    zeros[...] = jnp.zeros(zeros.shape, BF)
    for copy in loads:
        copy.wait()

    def start(part, carried):
        @pl.when(live_ref[part] > 0)
        def _():
            row = pl.multiple_of(blk_ref[part] * TILE, TILE)
            pltpu.make_async_copy(
                projected_ref.at[pl.ds(row, TILE)], outgoing_hbm.at[part], sems.at[part]
            ).start()

        @pl.when(live_ref[part] <= 0)
        def _():
            pltpu.make_async_copy(zeros, outgoing_hbm.at[part], sems.at[part]).start()

        return carried

    def wait(part, carried):
        pltpu.make_async_copy(zeros, outgoing_hbm.at[part], sems.at[part]).wait()
        return carried

    lax.fori_loop(0, parts, start, 0)
    lax.fori_loop(0, parts, wait, 0)


def spread_kernel(ring, blocks, pos_ref, count_ref, place_ref, tiles_ref, *outs):
    rows = blocks * TILE
    place = place_ref[0]
    for offset in range(ring):
        dense = outs[offset]
        dense[...] = jnp.zeros(dense.shape, BF)
        spot = lax.rem(place + offset, ring)
        for half in range(FAR):
            source = half * ring + spot

            def put(slot, carried, dense=dense, half=half, source=source):
                position = pos_ref[source * tiles_ref.shape[1] + slot]
                target = pl.multiple_of(position // blocks * TILE, TILE)
                origin = pl.multiple_of(half * rows + position % blocks * TILE, TILE)
                dense[pl.ds(target, TILE), pl.ds(origin, TILE)] = tiles_ref[source, slot]
                return carried

            lax.fori_loop(0, count_ref[source], put, 0)


def spread_cut_kernel(dst_ref, cut_ref, dense_hbm, dense, sem):
    chunks, _, columns = dense.shape
    chunk = columns // TILE
    dense[...] = jnp.zeros(dense.shape, BF)

    def put(part, carried):
        target = pl.multiple_of(dst_ref[part] * TILE, TILE)
        origin = pl.multiple_of(lax.rem(part, chunk) * TILE, TILE)
        dense[lax.div(part, chunk), pl.ds(target, TILE), pl.ds(origin, TILE)] = cut_ref[part]
        return carried

    lax.fori_loop(0, chunks * chunk, put, 0)
    copy = pltpu.make_async_copy(dense, dense_hbm, sem)
    copy.start()
    copy.wait()


def pair_kernel(half_ref, own_ref, other_ref, pair_ref):
    rows = own_ref.shape[0]
    place = pl.multiple_of(half_ref[0] * rows, TILE)
    pair_ref[pl.ds(place, rows)] = own_ref[...]
    pair_ref[pl.ds(pl.multiple_of(rows - place, TILE), rows)] = other_ref[...]


def cut_sum_kernel(cut_hbm, far_hbm, total_ref, cut, far, sems):
    chunks = cut.shape[0]
    chunk = far.shape[0] // chunks
    width = far.shape[2]
    copies = []
    for piece in range(chunks):
        span = pl.ds(piece * chunk, chunk)
        copies.append(
            (
                pltpu.make_async_copy(cut_hbm.at[piece], cut.at[piece], sems.at[piece]),
                pltpu.make_async_copy(far_hbm.at[span], far.at[span], sems.at[chunks + piece]),
            )
        )
    for pair in copies:
        for copy in pair:
            copy.start()
    for piece in range(chunks):
        for copy in copies[piece]:
            copy.wait()
        arrived = far[pl.ds(piece * chunk, chunk)].reshape(chunk * TILE, width)
        term = product(cut[piece], arrived)
        total_ref[...] = term if piece == 0 else total_ref[...] + term


def middle_kernel(
    sum_ref,
    cut_sum_ref,
    last_ref,
    bias_ref,
    cotangent_ref,
    far_mat_ref,
    near_mat_ref,
    cut_hbm,
    hidden_ref,
    grad_ref,
    left_hbm,
    right_hbm,
    terms_hbm,
    messages,
    cut,
    terms,
    sems,
):
    chunks = cut.shape[0]
    chunk = terms.shape[0] // chunks
    loads = [
        pltpu.make_async_copy(cut_hbm.at[piece], cut.at[piece], sems.at[piece])
        for piece in range(chunks)
    ]
    for copy in loads:
        copy.start()
    total = sum_ref[...] + cut_sum_ref[...] + product(far_mat_ref[...], last_ref[...])
    activated, derivative = silu_parts(total + bias_ref[...])
    hidden_ref[...] = activated.astype(BF)
    grad = (cotangent_ref[...].astype(F32) * derivative).T.astype(BF)
    grad_ref[...] = grad
    stores = []
    for place, (mat_ref, out_hbm) in enumerate(
        ((far_mat_ref, left_hbm), (near_mat_ref, right_hbm))
    ):
        messages[place] = product(grad, mat_ref[...]).astype(BF)
        stores.append(
            pltpu.make_async_copy(messages.at[place], out_hbm, sems.at[2 * chunks + place])
        )
        stores[-1].start()
    for piece in range(chunks):
        loads[piece].wait()
        result = product(grad, cut[piece]).astype(BF)
        for slot in range(chunk):
            terms[piece * chunk + slot] = result[:, slot * TILE : (slot + 1) * TILE]
        span = pl.ds(piece * chunk, chunk)
        stores.append(
            pltpu.make_async_copy(terms.at[span], terms_hbm.at[span], sems.at[chunks + piece])
        )
        stores[-1].start()
    for copy in stores:
        copy.wait()


def gather_kernel(blk_ref, live_ref, arrived_ref, total_ref):
    total_ref[...] = jnp.zeros(total_ref.shape, F32)

    def add(part, carried):
        @pl.when(live_ref[part] > 0)
        def _():
            columns = pl.ds(pl.multiple_of(blk_ref[part] * TILE, TILE), TILE)
            total_ref[:, columns] += arrived_ref[part].astype(F32)

        return carried

    lax.fori_loop(0, arrived_ref.shape[0], add, 0)


def hop_kernel(grad_ref, mat_ref, arrived_ref, out_ref):
    term = product(grad_ref[...], mat_ref[...]) + arrived_ref[...].astype(F32)
    out_ref[...] = term.astype(BF)


def close_kernel(
    half_ref, grad_ref, mat_ref, left_ref, right_ref, own_ref, upper_ref, lower_ref
):
    rows = grad_ref.shape[1]
    mine = pl.ds(pl.multiple_of(half_ref[0] * rows, TILE), rows)
    theirs = pl.ds(pl.multiple_of((1 - half_ref[0]) * rows, TILE), rows)

    def total(columns):
        arrived = left_ref[:, columns].astype(F32) + right_ref[:, columns].astype(F32)
        return product(grad_ref[...], mat_ref[:, columns]) + arrived

    middle = upper_ref.shape[0]
    other = total(theirs).astype(BF)
    upper_ref[...] = other[:middle]
    lower_ref[...] = other[middle:]
    own_ref[...] = total(mine)


def last_kernel(own_ref, upper_ref, lower_ref, cut_ref, weight_ref, out_ref):
    other = jnp.concatenate([upper_ref[...], lower_ref[...]]).astype(F32)
    total = own_ref[...] + other + cut_ref[...]
    out_ref[...] = lax.dot_general(
        total.T.astype(BF), weight_ref[...], (((1,), (1,)), ((), ())), preferred_element_type=F32
    ).astype(BF)


def on_device(
    features,
    weight,
    bias,
    cotangent,
    in_tiles,
    in_pos,
    in_count,
    cut_tiles,
    send_blk,
    send_live,
    recv_dst,
):
    rows, width = features.shape
    blocks = rows // TILE
    peers = lax.axis_size("blk")
    parts = lax.axis_size("dom")
    ring = peers // FAR
    reach = ring // 2
    me = lax.axis_index("blk")
    place, half = me % ring, me // ring
    wide = FAR * rows
    chunks = min(CHUNKS, parts)
    send_to, is_live, dst = send_blk[0, 0], send_live[0, 0], recv_dst[0, 0]
    shape = jax.ShapeDtypeStruct

    def along_ring(value, by):
        moves = [
            (side * ring + spot, side * ring + (spot + by) % ring)
            for side in range(FAR)
            for spot in range(ring)
        ]
        return lax.ppermute(value, "blk", moves)

    def across(value):
        return lax.ppermute(value, "blk", [(i, (i + ring) % peers) for i in range(peers)])

    projected = call(
        project_kernel,
        "project",
        shape((rows, width), BF),
        [HBM, HBM],
        VMEM,
        [
            pltpu.VMEM(features.shape, BF),
            pltpu.VMEM(weight.shape, BF),
            pltpu.SemaphoreType.DMA((2,)),
        ],
    )(in_hbm(features), in_hbm(weight))
    partner = across(projected)
    outgoing = call(
        fill_kernel,
        "fill",
        pltpu.HBM((parts, TILE, width), BF),
        [HBM, HBM, VMEM],
        HBM,
        [
            pltpu.SMEM((parts,), jnp.int32),
            pltpu.SMEM((parts,), jnp.int32),
            pltpu.VMEM((TILE, width), BF),
            pltpu.SemaphoreType.DMA((2,)),
            pltpu.SemaphoreType.DMA((parts,)),
        ],
    )(in_hbm(send_to), in_hbm(is_live), projected)
    incoming = lax.all_to_all(outgoing, "dom", split_axis=0, concat_axis=0, tiled=True)

    dense = call(
        lambda *refs: spread_kernel(ring, blocks, *refs),
        "spread",
        tuple([shape((rows, wide), BF)] * ring),
        [SMEM, SMEM, SMEM, VMEM],
        tuple([VMEM] * ring),
        moved=10 << 20,
    )(in_pos[0, 0].reshape(-1), in_count[0, 0], place.reshape(1), in_tiles[0, 0])
    dense_cut = call(
        spread_cut_kernel,
        "spread_cut",
        pltpu.HBM((chunks, rows, parts // chunks * TILE), BF),
        [SMEM, VMEM],
        HBM,
        [
            pltpu.VMEM((chunks, rows, parts // chunks * TILE), BF),
            pltpu.SemaphoreType.DMA,
        ],
        moved=6 << 20,
    )(dst, cut_tiles[0, 0])

    pair = call(
        pair_kernel, "pair", shape((wide, width), BF), [SMEM, VMEM, VMEM], VMEM, flops=PAIR_COST
    )(half.reshape(1), projected, partner)
    running = product(dense[0], pair)
    right = left = pair
    for hop in range(1, reach):
        right, left = along_ring(right, 1), along_ring(left, -1)
        running = running + product(dense[ring - hop], right)
        running = running + product(dense[hop], left)
    left = along_ring(left, -1)
    cut_sum = call(
        cut_sum_kernel,
        "cut_sum",
        shape((rows, width), F32),
        [HBM, HBM],
        VMEM,
        [
            pltpu.VMEM(dense_cut.shape, BF),
            pltpu.VMEM((parts, TILE, width), BF),
            pltpu.SemaphoreType.DMA((2 * chunks,)),
        ],
        flops=CUT_COST,
    )(in_hbm(dense_cut), in_hbm(incoming))

    hidden, grad_pre, left, right, terms = call(
        middle_kernel,
        "middle",
        (shape((rows, width), BF), shape((width, rows), BF))
        + (pltpu.HBM((width, wide), BF),) * 2
        + (pltpu.HBM((parts, width, TILE), BF),),
        [VMEM] * 7 + [HBM],
        (VMEM,) * 2 + (HBM,) * 3,
        [
            pltpu.VMEM((2, width, wide), BF),
            pltpu.VMEM(dense_cut.shape, BF),
            pltpu.VMEM((parts, width, TILE), BF),
            pltpu.SemaphoreType.DMA((2 * chunks + 2,)),
        ],
    )(
        running,
        cut_sum,
        left,
        bias.reshape(1, width),
        cotangent,
        dense[reach],
        dense[reach - 1],
        in_hbm(dense_cut),
    )

    def add_on(mat, arrived):
        return call(hop_kernel, "hop", shape((width, wide), BF), [VMEM] * 3, VMEM)(
            grad_pre, mat, arrived
        )

    left, right = along_ring(left, -1), along_ring(right, 1)
    returned = lax.all_to_all(terms, "dom", split_axis=0, concat_axis=0, tiled=True)
    for hop in range(reach - 1, 0, -1):
        left = along_ring(add_on(dense[ring - hop], left), -1)
        if hop > 1:
            right = along_ring(add_on(dense[hop - 1], right), 1)
    own, upper, lower = call(
        close_kernel,
        "close",
        (shape((width, rows), F32),) + (shape((width // 2, rows), BF),) * 2,
        [SMEM] + [VMEM] * 4,
        (VMEM,) * 3,
        flops=CLOSE_COST,
    )(half.reshape(1), grad_pre, dense[0], right, left)
    upper, lower = across(upper), across(lower)
    from_cuts = call(
        gather_kernel, "gather", shape((width, rows), F32), [SMEM, SMEM, VMEM], VMEM, moved=2 << 20
    )(send_to, is_live, returned)
    grad_features = call(
        last_kernel, "last", shape((rows, width), BF), [VMEM] * 5, VMEM
    )(own, upper, lower, from_cuts, weight)
    return (hidden, grad_features)


def solution(mesh):
    in_specs = (
        P(("dom", "blk"), None),
        P(),
        P(),
        P(("dom", "blk"), None),
        P("dom", "blk", None, None, None, None),
        P("dom", "blk", None, None),
        P("dom", "blk", None),
        P("dom", "blk", None, None, None),
        P("dom", "blk", None),
        P("dom", "blk", None),
        P("dom", "blk", None),
    )
    out_specs = (P(("dom", "blk"), None), P(("dom", "blk"), None))
    return jax.shard_map(
        on_device, mesh=mesh, in_specs=in_specs, out_specs=out_specs, check_vma=False
    )
```
